32 devices in a mesh: grp: 4 (over y, x), dap: 8 (over z, core).
Axes of the slice: x: 2, y: 2, z: 4, core: 2. Of those that a mesh axis runs over, the one named last changes fastest.
Arguments:
- pair_state: bfloat16 [8, 128, 128, 128], P('grp', 'dap'), may hold values from -6 to 6
- lengths: int32 [8], replicated, may hold values from 32 to 128, as said below
- norm_gain: float32 [3, 128], replicated, may hold values from 0.1 to 1.9
- norm_shift: float32 [3, 128], replicated, may hold values from -3 to 3
- attn_proj: bfloat16 [2, 128, 512], replicated
- bias_proj: bfloat16 [2, 128, 4], replicated, may hold values from -1.5 to 1.5
- attn_out: bfloat16 [2, 128, 128], replicated, may hold values from -0.5 to 0.5
- trans_up: bfloat16 [128, 512], replicated, may hold values from -0.5 to 0.5
- trans_down: bfloat16 [512, 128], replicated, may hold values from -0.25 to 0.25
Outputs:
- pair_out: bfloat16 [8, 128, 128, 128], P('grp', 'dap')
The draws below stay inside these ranges and needn't reach their ends.
Inputs may be any that keep to these rules, and one draw needn't show every extreme that they name: `lengths`: residues of each protein; one protein has exactly 128.
All inputs are finite; a program needn't handle non-finite values.
Results may differ from the reference program's by a relative error of at most 0.035.
Values may be sent and summed in bfloat16 or wider, within the bound.
A program may use at most 128 MiB of HBM per device.

```python
import jax
import jax.numpy as jnp
from jax import lax

PAIR = 128
HEADS = 4
HEAD_DIM = 32
TRANS = 512
PROTEINS = 8
RESIDUES = 128
ROW_BLOCK = 4


def draw_lengths(key, part):
    key = jax.random.fold_in(key, 11)
    first_key, second_key = jax.random.split(key)
    drawn = jax.random.randint(first_key, (PROTEINS,), RESIDUES // 4, RESIDUES + 1)
    longest = jax.random.randint(second_key, (), 0, PROTEINS)
    return jnp.where(jnp.arange(PROTEINS) == longest, RESIDUES, drawn).astype(jnp.int32)


def draw_attn_proj(key, part):
    key = jax.random.fold_in(key, 23)
    first_key = jax.random.fold_in(key, 0)
    values = jax.random.normal(first_key, (2, PAIR, 4 * PAIR), jnp.float32) * PAIR ** (-0.5)
    return values.astype(jnp.bfloat16)


def level_of(rng, extent, shards, smallest, top_value):
    gain = 1.0
    for position, blocks in shards:
        draws = jax.random.uniform(jax.random.fold_in(jax.random.fold_in(rng, 6), position), (blocks,), jnp.float32, smallest / len(shards), top_value / len(shards))
        gain = gain * jnp.repeat(jnp.exp(draws), extent[position] // blocks).reshape((-1,) + (1,) * (len(extent) - 1 - position))
    return gain


def bell_draw(key, shape, width, limit, cuts=(), kind=jnp.bfloat16):
    values = jax.random.normal(key, shape, jnp.float32) * width
    if len(cuts) > 0:
        values = level_of(key, shape, cuts, -0.22, 0.18) * values
    return jnp.clip(values, min=-limit, max=limit).astype(kind)


def setup_inputs(seed: int = 0) -> dict:
    streams_of = jax.random.split(jax.random.key(seed), 10)
    return {
        "pair_state": bell_draw(streams_of[0], (PROTEINS, RESIDUES, RESIDUES, PAIR), 1.0, 6.0, ((0, 4), (1, 8))),
        "lengths": draw_lengths(jax.random.fold_in(streams_of[9], 71), 0),
        "norm_gain": jnp.clip(1.0 + 0.18 * jax.random.normal(streams_of[2], (3, PAIR), jnp.float32), 0.1, 1.9),
        "norm_shift": bell_draw(streams_of[3], (3, PAIR), 0.5, 3.0, (), jnp.float32),
        "attn_proj": draw_attn_proj(jax.random.fold_in(streams_of[9], 71), 0),
        "bias_proj": bell_draw(streams_of[5], (2, PAIR, HEADS), (PAIR // 8) ** -0.5, 1.5),
        "attn_out": bell_draw(streams_of[6], (2, PAIR, PAIR), PAIR ** -0.5, 0.5),
        "trans_up": bell_draw(streams_of[7], (PAIR, TRANS), PAIR ** -0.5, 0.5),
        "trans_down": bell_draw(streams_of[8], (TRANS, PAIR), TRANS ** -0.5, 0.25),
    }


EPSILON = 1e-05
MASKED = -1000000000.0

def layer_norm(values, gain_row, shift_row):
    values = values.astype(jnp.float32)
    center = values - lax.optimization_barrier(jnp.mean(values, -1, keepdims=True))
    spread = lax.optimization_barrier(jnp.mean(center * center, -1, keepdims=True))
    return (center * lax.rsqrt(spread + EPSILON) * gain_row + shift_row).astype(jnp.bfloat16)

def block_update(normed, bias_full, length, start, proj_in, proj_out):
    width_all = normed.shape[1]
    chans = normed.shape[2]
    rows_in = lax.dynamic_slice_in_dim(normed, start, ROW_BLOCK, 0)
    projected = jnp.dot(rows_in.reshape(-1, chans), proj_in, preferred_element_type=jnp.float32)
    projected = projected.reshape(ROW_BLOCK, width_all, 4 * chans)
    query = (projected[..., :chans] * HEAD_DIM ** (-0.5)).astype(jnp.bfloat16).reshape(ROW_BLOCK, width_all, HEADS, HEAD_DIM)
    keyed = projected[..., chans:2 * chans].astype(jnp.bfloat16).reshape(ROW_BLOCK, width_all, HEADS, HEAD_DIM)
    valued = projected[..., 2 * chans:3 * chans].astype(jnp.bfloat16).reshape(ROW_BLOCK, width_all, HEADS, HEAD_DIM)
    gating = projected[..., 3 * chans:]
    scores = jnp.einsum('rjhd,rkhd->rhjk', query.astype(jnp.float32), keyed.astype(jnp.float32))
    scores = scores + bias_full.astype(jnp.float32)[None]
    live = jnp.arange(width_all, dtype=jnp.int32) < length
    scores = jnp.where(live, scores, MASKED)
    weights = jax.nn.softmax(scores, axis=-1).astype(jnp.bfloat16)
    mixed = jnp.einsum('rhjk,rkhd->rjhd', weights.astype(jnp.float32), valued.astype(jnp.float32))
    mixed = mixed.reshape(ROW_BLOCK, width_all, chans)
    gated = (mixed * jax.nn.sigmoid(gating)).astype(jnp.bfloat16)
    result = jnp.dot(gated.reshape(-1, chans), proj_out, preferred_element_type=jnp.float32)
    return result.reshape(ROW_BLOCK, width_all, chans)

def cell_mask(width_all, length):
    live = jnp.arange(width_all, dtype=jnp.int32) < length
    return (live[:, None] & live[None, :])[..., None]

def row_module(pair, length, gain_row, shift_row, proj_in, proj_bias, proj_out):
    width_all = pair.shape[0]
    normed = layer_norm(pair, gain_row, shift_row)
    bias_full = jnp.einsum('jkc,ch->hjk', normed.astype(jnp.float32), proj_bias.astype(jnp.float32)).astype(jnp.bfloat16)

    def one_block(start):
        return block_update(normed, bias_full, length, start, proj_in, proj_out)
    starts = jnp.arange(0, width_all, ROW_BLOCK, dtype=jnp.int32)
    update = lax.map(one_block, starts).reshape(pair.shape)
    update = jnp.where(cell_mask(width_all, length), update, 0.0)
    return (pair.astype(jnp.float32) + update).astype(jnp.bfloat16)

def transition(pair, length, gain_row, shift_row, up_proj, down_proj):
    width_all = pair.shape[0]
    chans = pair.shape[2]
    normed = layer_norm(pair, gain_row, shift_row)

    def one_block(start):
        rows_in = lax.dynamic_slice_in_dim(normed, start, ROW_BLOCK, 0)
        hidden_units = jax.nn.relu(jnp.dot(rows_in.reshape(-1, chans), up_proj, preferred_element_type=jnp.float32)).astype(jnp.bfloat16)
        result = jnp.dot(hidden_units, down_proj, preferred_element_type=jnp.float32)
        return result.reshape(ROW_BLOCK, width_all, chans)
    starts = jnp.arange(0, width_all, ROW_BLOCK, dtype=jnp.int32)
    update = lax.map(one_block, starts).reshape(pair.shape)
    update = jnp.where(cell_mask(width_all, length), update, 0.0)
    return (pair.astype(jnp.float32) + update).astype(jnp.bfloat16)

def reference(pair_state, lengths, norm_gain, norm_shift, attn_proj, bias_proj, attn_out, trans_up, trans_down):

    def protein(operands):
        pair, length = operands
        first = row_module(pair, length, norm_gain[0], norm_shift[0], attn_proj[0], bias_proj[0], attn_out[0])
        flipped = row_module(jnp.swapaxes(first, 0, 1), length, norm_gain[1], norm_shift[1], attn_proj[1], bias_proj[1], attn_out[1])
        second = jnp.swapaxes(flipped, 0, 1)
        return transition(second, length, norm_gain[2], norm_shift[2], trans_up, trans_down)
    return lax.map(protein, (pair_state, lengths))
```

```python
from functools import partial

import jax
import jax.numpy as jnp
from jax import lax
from jax.experimental import pallas as pl
from jax.experimental.pallas import tpu as pltpu
from jax.sharding import PartitionSpec as P

HEADS = 4
HEAD_DIM = 32
EPSILON = 1e-05
MASKED = -1e30
JBLOCK = 128

NT = (((1,), (1,)), ((), ()))


def layer_norm(values, gain_row, shift_row):
    values = values.astype(jnp.float32)
    center = values - jnp.mean(values, -1, keepdims=True)
    spread = jnp.mean(center * center, -1, keepdims=True)
    return (center * lax.rsqrt(spread + EPSILON) * gain_row + shift_row).astype(jnp.bfloat16)


def dot32(left, right):
    return jnp.dot(left, right, preferred_element_type=jnp.float32)


def kernel(
    dims,
    lens_ref,
    x_ref,
    gain_ref,
    shift_ref,
    proj_ref,
    wb_ref,
    wo_ref,
    up_ref,
    down_ref,
    out_ref,
    x1,
    y_s,
    q_s,
    k_s,
    v_s,
    g_s,
    tsc,
    bsc,
    bias_s,
    send_s,
    bias_send,
    bias_recv,
    flip_send,
    flip_recv,
):
    count, G, R, W, C, RB = dims
    me = lax.axis_index("dap")
    grp = lax.axis_index("grp")
    first_row = me * R
    my_cols = pl.ds(pl.multiple_of(first_row, R), R)

    barrier = pltpu.get_barrier_semaphore()

    def greet(d, carry):
        pl.semaphore_signal(
            barrier,
            inc=1,
            device_id=(grp, lax.rem(me + d, count)),
            device_id_type=pl.DeviceIdType.MESH,
        )
        return carry

    lax.fori_loop(1, count, greet, 0)

    lens = [lens_ref[grp * G + g] for g in range(G)]

    def bias_copy(m, g, d):
        return pltpu.make_async_remote_copy(
            src_ref=bias_s.at[m, me, g],
            dst_ref=bias_s.at[m, me, g],
            send_sem=bias_send.at[m, g, d],
            recv_sem=bias_recv.at[m, g, d],
            device_id=(grp, lax.rem(me + d, count)),
            device_id_type=pl.DeviceIdType.MESH,
        )

    def flip_copy(m, g, d):
        peer = lax.rem(me + d, count)
        land = x1 if m == 0 else out_ref
        return pltpu.make_async_remote_copy(
            src_ref=send_s.at[g, peer],
            dst_ref=land.at[g, :, my_cols, :],
            send_sem=flip_send.at[m, g, d],
            recv_sem=flip_recv.at[m, g, d],
            device_id=(grp, peer),
            device_id_type=pl.DeviceIdType.MESH,
        )

    def each_peer(act):
        def one(d, carry):
            act(d)
            return carry

        lax.fori_loop(1, count, one, 0)

    def norm_bias(m, g, src):
        gain = gain_ref[m : m + 1, :]
        shift = shift_ref[m : m + 1, :]

        def chunk(b, carry):
            rows = pl.ds(b * RB, RB)
            y = layer_norm(src[g, rows].reshape(RB * W, C), gain, shift)
            y_s[g, rows] = y.reshape(RB, W, C)
            bias = lax.dot_general(wb_ref[m], y, NT, preferred_element_type=jnp.float32)
            for rr in range(RB):
                bsc[b * RB + rr] = bias[:, rr * W : (rr + 1) * W]
            return carry

        lax.fori_loop(0, R // RB, chunk, 0)
        live = lax.broadcasted_iota(jnp.int32, (R, W), 1) < lens[g]
        for h in range(HEADS):
            bias_s[m, me, g, h] = jnp.where(live, bsc[:, h, :], MASKED).astype(jnp.bfloat16)

    def project(m, g):
        def chunk(b, carry):
            rows = pl.ds(b * RB, RB)
            y = y_s[g, rows].reshape(RB * W, C)
            p = dot32(y, proj_ref[m])
            q_s[rows] = (p[:, :C] * HEAD_DIM ** (-0.5)).astype(jnp.bfloat16).reshape(RB, W, C)
            k_s[rows] = p[:, C : 2 * C].astype(jnp.bfloat16).reshape(RB, W, C)
            v_s[rows] = p[:, 2 * C : 3 * C].astype(jnp.bfloat16).reshape(RB, W, C)
            g_s[rows] = jax.nn.sigmoid(p[:, 3 * C :]).reshape(RB, W, C)
            return carry

        lax.fori_loop(0, R // RB, chunk, 0)

    def row_mixed(m, g, r):
        head = lax.broadcasted_iota(jnp.int32, (JBLOCK, C), 1) // HEAD_DIM
        k = k_s[r]
        vext = jnp.concatenate([v_s[r], jnp.ones((W, C), jnp.bfloat16)], axis=1)
        per = JBLOCK // R
        parts = []
        for jb in range(W // JBLOCK):
            q = q_s[r, jb * JBLOCK : (jb + 1) * JBLOCK, :]
            stacked = jnp.concatenate(
                [jnp.where(head == h, q, jnp.zeros_like(q)) for h in range(HEADS)], axis=0
            )
            scores = lax.dot_general(stacked, k, NT, preferred_element_type=jnp.float32)
            weights = []
            for h in range(HEADS):
                bias = bias_s[m, jb * per : (jb + 1) * per, g, h].reshape(JBLOCK, W)
                s = scores[h * JBLOCK : (h + 1) * JBLOCK] + bias.astype(jnp.float32)
                top = jnp.max(s, -1, keepdims=True)
                weights.append(jnp.exp(s - top).astype(jnp.bfloat16))
            summed = dot32(jnp.concatenate(weights, axis=0), vext)
            num = summed[:JBLOCK, :C]
            den = summed[:JBLOCK, C:]
            for h in range(1, HEADS):
                at = slice(h * JBLOCK, (h + 1) * JBLOCK)
                num = jnp.where(head == h, summed[at, :C], num)
                den = jnp.where(head == h, summed[at, C:], den)
            parts.append(num / den)
        mixed = parts[0] if len(parts) == 1 else jnp.concatenate(parts, axis=0)
        return (mixed * g_s[r]).astype(jnp.bfloat16)

    def attend(m, g, src):
        col = lax.broadcasted_iota(jnp.int32, (W, C), 0)

        def live_of(r):
            return col < jnp.where(first_row + r < lens[g], lens[g], 0)

        def chunk(b, carry):
            gated = [row_mixed(m, g, b * RB + rr) for rr in range(RB)]
            joined = gated[0] if RB == 1 else jnp.concatenate(gated, axis=0)
            update = dot32(joined, wo_ref[m])
            done = []
            for rr in range(RB):
                r = b * RB + rr
                u = jnp.where(live_of(r), update[rr * W : (rr + 1) * W], 0.0)
                done.append((src[g, r].astype(jnp.float32) + u).astype(jnp.bfloat16))
            if m == 1:
                second = done[0] if RB == 1 else jnp.concatenate(done, axis=0)
                y = layer_norm(second, gain_ref[2:3, :], shift_ref[2:3, :])
                hidden = jnp.maximum(dot32(y, up_ref[...]), 0.0).astype(jnp.bfloat16)
                update = dot32(hidden, down_ref[...])
                for rr in range(RB):
                    r = b * RB + rr
                    u = jnp.where(live_of(r), update[rr * W : (rr + 1) * W], 0.0)
                    done[rr] = (done[rr].astype(jnp.float32) + u).astype(jnp.bfloat16)
            for rr in range(RB):
                tsc[:, b * RB + rr] = done[rr].astype(jnp.float32).reshape(W // R, R, C)
            return carry

        lax.fori_loop(0, R // RB, chunk, 0)

    def flip(m, g):
        if m == 1:
            each_peer(lambda d: flip_copy(0, g, d).wait_send())
        land = x1 if m == 0 else out_ref

        def one(d):
            peer = lax.rem(me + d, count)
            for c in range(R):
                send_s[g, peer, c] = tsc[peer, :, c, :].astype(jnp.bfloat16)
            flip_copy(m, g, d).start()

        each_peer(one)
        for c in range(R):
            land[g, c, my_cols, :] = tsc[me, :, c, :].astype(jnp.bfloat16)

    for g in range(G):
        norm_bias(0, g, x_ref)
        if g == 0:
            pl.semaphore_wait(barrier, count - 1)
        each_peer(lambda d: bias_copy(0, g, d).start())
    for g in range(G):
        project(0, g)
        each_peer(lambda d: bias_copy(0, g, d).wait_recv())
        attend(0, g, x_ref)
        flip(0, g)
    for g in range(G):
        each_peer(lambda d: flip_copy(0, g, d).wait_recv())
        norm_bias(1, g, x1)
        each_peer(lambda d: bias_copy(1, g, d).start())
    for g in range(G):
        project(1, g)
        each_peer(lambda d: bias_copy(1, g, d).wait_recv())
        attend(1, g, x1)
        flip(1, g)
    for g in range(G):
        each_peer(lambda d: flip_copy(1, g, d).wait())
        for m in range(2):
            each_peer(lambda d: bias_copy(m, g, d).wait_send())


def on_device(
    pair_state, lengths, norm_gain, norm_shift, attn_proj, bias_proj, attn_out, trans_up, trans_down
):
    G, R, W, C = pair_state.shape
    count = lax.axis_size("dap")
    RB = 4 if W <= 128 else 1
    wb = jnp.pad(jnp.swapaxes(bias_proj, 1, 2), ((0, 0), (0, 8 - HEADS), (0, 0)))
    bf = jnp.bfloat16
    f32 = jnp.float32
    vm = pl.BlockSpec(memory_space=pltpu.VMEM)
    return pl.pallas_call(
        partial(kernel, (count, G, R, W, C, RB)),
        out_shape=jax.ShapeDtypeStruct((G, R, W, C), bf),
        in_specs=[pl.BlockSpec(memory_space=pltpu.SMEM)] + [vm] * 8,
        out_specs=vm,
        scratch_shapes=[
            pltpu.VMEM((G, R, W, C), bf),
            pltpu.VMEM((G, R, W, C), bf),
            pltpu.VMEM((R, W, C), bf),
            pltpu.VMEM((R, W, C), bf),
            pltpu.VMEM((R, W, C), bf),
            pltpu.VMEM((R, W, C), f32),
            pltpu.VMEM((count, R, R, C), f32),
            pltpu.VMEM((R, 8, W), f32),
            pltpu.VMEM((2, count, G, HEADS, R, W), bf),
            pltpu.VMEM((G, count, R, R, C), bf),
            pltpu.SemaphoreType.DMA((2, G, count)),
            pltpu.SemaphoreType.DMA((2, G, count)),
            pltpu.SemaphoreType.DMA((2, G, count)),
            pltpu.SemaphoreType.DMA((2, G, count)),
        ],
        compiler_params=pltpu.CompilerParams(
            collective_id=0, has_side_effects=True, vmem_limit_bytes=60 * 1024 * 1024
        ),
        name="evoformer_pair",
    )(lengths, pair_state, norm_gain, norm_shift, attn_proj, wb, attn_out, trans_up, trans_down)


def solution(mesh):
    in_specs = (P("grp", "dap", None, None), P(), P(), P(), P(), P(), P(), P(), P())
    out_specs = P("grp", "dap", None, None)
    return jax.shard_map(
        on_device, mesh=mesh, in_specs=in_specs, out_specs=out_specs, check_vma=False
    )
```

```python
from functools import partial

import jax
import jax.numpy as jnp
from jax import lax
from jax.experimental import pallas as pl
from jax.experimental.pallas import tpu as pltpu
from jax.sharding import PartitionSpec as P

HEADS = 4
HEAD_DIM = 32
EPSILON = 1e-05
MASKED = -1e30
JBLOCK = 128

NT = (((1,), (1,)), ((), ()))


def layer_norm(values, gain_row, shift_row):
    values = values.astype(jnp.float32)
    center = values - jnp.mean(values, -1, keepdims=True)
    spread = jnp.mean(center * center, -1, keepdims=True)
    return (center * lax.rsqrt(spread + EPSILON) * gain_row + shift_row).astype(jnp.bfloat16)


def dot32(left, right):
    return jnp.dot(left, right, preferred_element_type=jnp.float32)


def kernel(
    dims,
    lens_ref,
    x_ref,
    gain_ref,
    shift_ref,
    proj_ref,
    wb_ref,
    wo_ref,
    up_ref,
    down_ref,
    out_ref,
    x1,
    landed,
    y_s,
    q_s,
    k_s,
    v_s,
    g_s,
    tsc,
    bsc,
    bias_s,
    send_s,
    bias_send,
    bias_recv,
    flip_send,
    flip_recv,
):
    count, G, R, W, C, RB = dims
    me = lax.axis_index("dap")
    grp = lax.axis_index("grp")
    first_row = me * R

    barrier = pltpu.get_barrier_semaphore()

    def greet(d, carry):
        pl.semaphore_signal(
            barrier,
            inc=1,
            device_id=(grp, lax.rem(me + d, count)),
            device_id_type=pl.DeviceIdType.MESH,
        )
        return carry

    lax.fori_loop(1, count, greet, 0)

    lens = [lens_ref[grp * G + g] for g in range(G)]

    def bias_copy(m, g, d):
        return pltpu.make_async_remote_copy(
            src_ref=bias_s.at[m, me, g],
            dst_ref=bias_s.at[m, me, g],
            send_sem=bias_send.at[m, g, d],
            recv_sem=bias_recv.at[m, g, d],
            device_id=(grp, lax.rem(me + d, count)),
            device_id_type=pl.DeviceIdType.MESH,
        )

    def flip_copy(m, g, d, start, size):
        peer = lax.rem(me + d, count)
        return pltpu.make_async_remote_copy(
            src_ref=send_s.at[g, pl.ds(start, size), peer],
            dst_ref=landed.at[m, g, pl.ds(first_row + start, size)],
            send_sem=flip_send.at[m, g, d],
            recv_sem=flip_recv.at[m, g, d],
            device_id=(grp, peer),
            device_id_type=pl.DeviceIdType.MESH,
        )

    def each_peer(act):
        def one(d, carry):
            act(d)
            return carry

        lax.fori_loop(1, count, one, 0, unroll=count <= 8)

    def norm_bias(m, g, src):
        gain = gain_ref[m : m + 1, :]
        shift = shift_ref[m : m + 1, :]
        pick = lax.broadcasted_iota(jnp.int32, (8, HEADS), 0) == lax.broadcasted_iota(
            jnp.int32, (8, HEADS), 1
        )
        wb = lax.dot_general(
            jnp.where(pick, 1.0, 0.0).astype(jnp.bfloat16),
            wb_ref[m],
            NT,
            preferred_element_type=jnp.float32,
        ).astype(jnp.bfloat16)

        def chunk(b, carry):
            rows = pl.ds(b * RB, RB)
            y = layer_norm(src[g, rows].reshape(RB * W, C), gain, shift)
            y_s[g, rows] = y.reshape(RB, W, C)
            bias = lax.dot_general(wb, y, NT, preferred_element_type=jnp.float32)
            for rr in range(RB):
                bsc[b * RB + rr] = bias[:, rr * W : (rr + 1) * W]
            return carry

        lax.fori_loop(0, R // RB, chunk, 0)
        live = lax.broadcasted_iota(jnp.int32, (R, W), 1) < lens[g]
        for h in range(HEADS):
            bias_s[m, me, g, h] = jnp.where(live, bsc[:, h, :], MASKED).astype(jnp.bfloat16)

    def project(m, g):
        def chunk(b, carry):
            rows = pl.ds(b * RB, RB)
            y = y_s[g, rows].reshape(RB * W, C)
            p = dot32(y, proj_ref[m])
            q_s[rows] = (p[:, :C] * HEAD_DIM ** (-0.5)).astype(jnp.bfloat16).reshape(RB, W, C)
            k_s[rows] = p[:, C : 2 * C].astype(jnp.bfloat16).reshape(RB, W, C)
            v_s[rows] = p[:, 2 * C : 3 * C].astype(jnp.bfloat16).reshape(RB, W, C)
            g_s[rows] = jax.nn.sigmoid(p[:, 3 * C :]).reshape(RB, W, C)
            return carry

        lax.fori_loop(0, R // RB, chunk, 0)

    def row_mixed(m, g, r):
        head = lax.broadcasted_iota(jnp.int32, (JBLOCK, C), 1) // HEAD_DIM
        k = k_s[r]
        vext = jnp.concatenate([v_s[r], jnp.ones((W, C), jnp.bfloat16)], axis=1)
        per = JBLOCK // R
        parts = []
        for jb in range(W // JBLOCK):
            q = q_s[r, jb * JBLOCK : (jb + 1) * JBLOCK, :]
            stacked = jnp.concatenate(
                [jnp.where(head == h, q, jnp.zeros_like(q)) for h in range(HEADS)], axis=0
            )
            scores = lax.dot_general(stacked, k, NT, preferred_element_type=jnp.float32)
            weights = []
            for h in range(HEADS):
                bias = bias_s[m, jb * per : (jb + 1) * per, g, h].reshape(JBLOCK, W)
                s = scores[h * JBLOCK : (h + 1) * JBLOCK] + bias.astype(jnp.float32)
                top = jnp.max(s, -1, keepdims=True)
                weights.append(jnp.exp(s - top).astype(jnp.bfloat16))
            summed = dot32(jnp.concatenate(weights, axis=0), vext)
            num = summed[:JBLOCK, :C]
            den = summed[:JBLOCK, C:]
            for h in range(1, HEADS):
                at = slice(h * JBLOCK, (h + 1) * JBLOCK)
                num = jnp.where(head == h, summed[at, :C], num)
                den = jnp.where(head == h, summed[at, C:], den)
            parts.append(num / den)
        mixed = parts[0] if len(parts) == 1 else jnp.concatenate(parts, axis=0)
        return (mixed * g_s[r]).astype(jnp.bfloat16)

    def attend(m, g, src):
        col = lax.broadcasted_iota(jnp.int32, (W, C), 0)

        def live_of(r):
            return col < jnp.where(first_row + r < lens[g], lens[g], 0)

        def chunk(b, carry):
            gated = [row_mixed(m, g, b * RB + rr) for rr in range(RB)]
            joined = gated[0] if RB == 1 else jnp.concatenate(gated, axis=0)
            update = dot32(joined, wo_ref[m])
            done = []
            for rr in range(RB):
                r = b * RB + rr
                u = jnp.where(live_of(r), update[rr * W : (rr + 1) * W], 0.0)
                done.append((src[g, r].astype(jnp.float32) + u).astype(jnp.bfloat16))
            if m == 1:
                second = done[0] if RB == 1 else jnp.concatenate(done, axis=0)
                y = layer_norm(second, gain_ref[2:3, :], shift_ref[2:3, :])
                hidden = jnp.maximum(dot32(y, up_ref[...]), 0.0).astype(jnp.bfloat16)
                update = dot32(hidden, down_ref[...])
                for rr in range(RB):
                    r = b * RB + rr
                    u = jnp.where(live_of(r), update[rr * W : (rr + 1) * W], 0.0)
                    done[rr] = (done[rr].astype(jnp.float32) + u).astype(jnp.bfloat16)
            for rr in range(RB):
                r = b * RB + rr
                send_s[g, r] = done[rr].reshape(count, R, C)
                landed[m, g, first_row + r] = send_s[g, r, me]
            each_peer(lambda d: flip_copy(m, g, d, b * RB, RB).start())
            return carry

        lax.fori_loop(0, R // RB, chunk, 0)

    def gather_flip(m, g, target):
        each_peer(lambda d: flip_copy(m, g, d, 0, R).wait_recv())

        def one(p, carry):
            rows = pl.ds(pl.multiple_of(p * R, R), R)
            tsc[p] = landed[m, g, rows].astype(jnp.float32)
            for c in range(R):
                target[g, c, rows, :] = tsc[p, :, c, :].astype(jnp.bfloat16)
            return carry

        lax.fori_loop(0, count, one, 0, unroll=count <= 8)

    for g in range(G):
        norm_bias(0, g, x_ref)
        if g == 0:
            pl.semaphore_wait(barrier, count - 1)
        each_peer(lambda d: bias_copy(0, g, d).start())
    for g in range(G):
        project(0, g)
        each_peer(lambda d: bias_copy(0, g, d).wait_recv())
        attend(0, g, x_ref)
    gather_flip(0, 0, x1)
    norm_bias(1, 0, x1)
    each_peer(lambda d: bias_copy(1, 0, d).start())
    project(1, 0)
    for g in range(1, G):
        gather_flip(0, g, x1)
        norm_bias(1, g, x1)
        each_peer(lambda d: bias_copy(1, g, d).start())
    for g in range(G):
        if g > 0:
            project(1, g)
        each_peer(lambda d: bias_copy(1, g, d).wait_recv())
        each_peer(lambda d: flip_copy(0, g, d, 0, R).wait_send())
        attend(1, g, x1)
    for g in range(G):
        gather_flip(1, g, out_ref)
        each_peer(lambda d: flip_copy(1, g, d, 0, R).wait_send())
        for m in range(2):
            each_peer(lambda d: bias_copy(m, g, d).wait_send())


def on_device(
    pair_state, lengths, norm_gain, norm_shift, attn_proj, bias_proj, attn_out, trans_up, trans_down
):
    G, R, W, C = pair_state.shape
    count = lax.axis_size("dap")
    RB = 4 if W <= 128 else 1
    bf = jnp.bfloat16
    f32 = jnp.float32
    vm = pl.BlockSpec(memory_space=pltpu.VMEM)
    return pl.pallas_call(
        partial(kernel, (count, G, R, W, C, RB)),
        out_shape=jax.ShapeDtypeStruct((G, R, W, C), bf),
        in_specs=[pl.BlockSpec(memory_space=pltpu.SMEM)] + [vm] * 8,
        out_specs=vm,
        scratch_shapes=[
            pltpu.VMEM((G, R, W, C), bf),
            pltpu.VMEM((2, G, W, R, C), bf),
            pltpu.VMEM((G, R, W, C), bf),
            pltpu.VMEM((R, W, C), bf),
            pltpu.VMEM((R, W, C), bf),
            pltpu.VMEM((R, W, C), bf),
            pltpu.VMEM((R, W, C), f32),
            pltpu.VMEM((count, R, R, C), f32),
            pltpu.VMEM((R, 8, W), f32),
            pltpu.VMEM((2, count, G, HEADS, R, W), bf),
            pltpu.VMEM((G, R, count, R, C), bf),
            pltpu.SemaphoreType.DMA((2, G, count)),
            pltpu.SemaphoreType.DMA((2, G, count)),
            pltpu.SemaphoreType.DMA((2, G, count)),
            pltpu.SemaphoreType.DMA((2, G, count)),
        ],
        compiler_params=pltpu.CompilerParams(
            collective_id=0, has_side_effects=True, vmem_limit_bytes=60 * 1024 * 1024
        ),
        name="evoformer_pair",
    )(lengths, pair_state, norm_gain, norm_shift, attn_proj, bias_proj, attn_out, trans_up, trans_down)


def solution(mesh):
    in_specs = (P("grp", "dap", None, None), P(), P(), P(), P(), P(), P(), P(), P())
    out_specs = P("grp", "dap", None, None)
    return jax.shard_map(
        on_device, mesh=mesh, in_specs=in_specs, out_specs=out_specs, check_vma=False
    )
```

```python
from functools import partial

import jax
import jax.numpy as jnp
from jax import lax
from jax.experimental import pallas as pl
from jax.experimental.pallas import tpu as pltpu
from jax.sharding import PartitionSpec as P

HEADS = 4
HEAD_DIM = 32
EPSILON = 1e-05
MASKED = -1e30
JBLOCK = 128

NT = (((1,), (1,)), ((), ()))


def layer_norm(values, gain_row, shift_row):
    values = values.astype(jnp.float32)
    center = values - jnp.mean(values, -1, keepdims=True)
    spread = jnp.mean(center * center, -1, keepdims=True)
    return (center * lax.rsqrt(spread + EPSILON) * gain_row + shift_row).astype(jnp.bfloat16)


def dot32(left, right):
    return jnp.dot(left, right, preferred_element_type=jnp.float32)


def kernel(
    dims,
    lens_ref,
    x_ref,
    gain_ref,
    shift_ref,
    proj_ref,
    wb_ref,
    wo_ref,
    up_ref,
    down_ref,
    out_ref,
    x1,
    landed,
    y_s,
    q_s,
    k_s,
    v_s,
    g_s,
    tsc,
    bsc,
    bias_t,
    bias_s,
    send_s,
    bias_send,
    bias_recv,
    flip_send,
    flip_recv,
):
    count, G, R, W, C, RB = dims
    me = lax.axis_index("dap")
    grp = lax.axis_index("grp")
    first_row = me * R

    barrier = pltpu.get_barrier_semaphore()

    def greet(d, carry):
        pl.semaphore_signal(
            barrier,
            inc=1,
            device_id=(grp, lax.rem(me + d, count)),
            device_id_type=pl.DeviceIdType.MESH,
        )
        return carry

    lax.fori_loop(1, count, greet, 0)

    pick = lax.broadcasted_iota(jnp.int32, (8, HEADS), 0) == lax.broadcasted_iota(
        jnp.int32, (8, HEADS), 1
    )
    pick = jnp.where(pick, 1.0, 0.0).astype(jnp.bfloat16)

    def length_of(g):
        return lens_ref[grp * G + g]

    def head_weights(m):
        return dot32(pick, wb_ref[m]).astype(jnp.bfloat16)

    def put_bias(weights, y, b):
        bias = lax.dot_general(weights, y, NT, preferred_element_type=jnp.float32)
        for rr in range(RB):
            bsc[b * RB + rr] = bias[:, rr * W : (rr + 1) * W]

    def send_bias(m, g, live):
        for h in range(HEADS):
            bias_s[m, me, g, h] = jnp.where(live, bsc[:, h, :], MASKED).astype(jnp.bfloat16)
        each_peer(lambda d: bias_copy(m, g, d).start())

    def bias_copy(m, g, d):
        return pltpu.make_async_remote_copy(
            src_ref=bias_s.at[m, me, g],
            dst_ref=bias_s.at[m, me, g],
            send_sem=bias_send.at[m, g, d],
            recv_sem=bias_recv.at[m, g, d],
            device_id=(grp, lax.rem(me + d, count)),
            device_id_type=pl.DeviceIdType.MESH,
        )

    def flip_copy(m, g, d, start, size):
        peer = lax.rem(me + d, count)
        return pltpu.make_async_remote_copy(
            src_ref=send_s.at[g, pl.ds(start, size), peer],
            dst_ref=landed.at[m, g, pl.ds(first_row + start, size)],
            send_sem=flip_send.at[m, g, d],
            recv_sem=flip_recv.at[m, g, d],
            device_id=(grp, peer),
            device_id_type=pl.DeviceIdType.MESH,
        )

    def each_peer(act):
        def one(d, carry):
            act(d)
            return carry

        lax.fori_loop(1, count, one, 0, unroll=count <= 8)

    def norm_bias(g):
        weights = head_weights(0)

        def chunk(b, carry):
            rows = pl.ds(b * RB, RB)
            y = layer_norm(x_ref[g, rows].reshape(RB * W, C), gain_ref[0:1, :], shift_ref[0:1, :])
            y_s[g, rows] = y.reshape(RB, W, C)
            put_bias(weights, y, b)
            return carry

        lax.fori_loop(0, R // RB, chunk, 0)

    def project(m, g):
        def chunk(b, carry):
            rows = pl.ds(b * RB, RB)
            if m == 0:
                y = y_s[g, rows].reshape(RB * W, C)
            else:
                y = layer_norm(
                    x1[g, rows].reshape(RB * W, C), gain_ref[1:2, :], shift_ref[1:2, :]
                )
            p = dot32(y, proj_ref[m])
            q_s[rows] = (p[:, :C] * HEAD_DIM ** (-0.5)).astype(jnp.bfloat16).reshape(RB, W, C)
            k_s[rows] = p[:, C : 2 * C].astype(jnp.bfloat16).reshape(RB, W, C)
            v_s[rows] = p[:, 2 * C : 3 * C].astype(jnp.bfloat16).reshape(RB, W, C)
            g_s[rows] = jax.nn.sigmoid(p[:, 3 * C :]).reshape(RB, W, C)
            return carry

        lax.fori_loop(0, R // RB, chunk, 0)

    def turn_bias(g):
        per = JBLOCK // R
        for h in range(HEADS):
            for kb in range(W // JBLOCK):
                part = bias_s[1, kb * per : (kb + 1) * per, g, h].reshape(JBLOCK, W)
                bias_t[h, :, kb * JBLOCK : (kb + 1) * JBLOCK] = part.astype(jnp.float32).T.astype(
                    jnp.bfloat16
                )

    def row_mixed(m, g, r):
        head = lax.broadcasted_iota(jnp.int32, (JBLOCK, C), 1) // HEAD_DIM
        k = k_s[r]
        vext = jnp.concatenate([v_s[r], jnp.ones((W, C), jnp.bfloat16)], axis=1)
        per = JBLOCK // R
        parts = []
        for jb in range(W // JBLOCK):
            q = q_s[r, jb * JBLOCK : (jb + 1) * JBLOCK, :]
            stacked = jnp.concatenate(
                [jnp.where(head == h, q, jnp.zeros_like(q)) for h in range(HEADS)], axis=0
            )
            scores = lax.dot_general(stacked, k, NT, preferred_element_type=jnp.float32)
            weights = []
            for h in range(HEADS):
                if m == 0:
                    bias = bias_s[0, jb * per : (jb + 1) * per, g, h].reshape(JBLOCK, W)
                else:
                    bias = bias_t[h, jb * JBLOCK : (jb + 1) * JBLOCK, :]
                s = scores[h * JBLOCK : (h + 1) * JBLOCK] + bias.astype(jnp.float32)
                top = jnp.max(s, -1, keepdims=True)
                weights.append(jnp.exp(s - top).astype(jnp.bfloat16))
            summed = dot32(jnp.concatenate(weights, axis=0), vext)
            num = summed[:JBLOCK, :C]
            den = summed[:JBLOCK, C:]
            for h in range(1, HEADS):
                at = slice(h * JBLOCK, (h + 1) * JBLOCK)
                num = jnp.where(head == h, summed[at, :C], num)
                den = jnp.where(head == h, summed[at, C:], den)
            parts.append(num / den)
        mixed = parts[0] if len(parts) == 1 else jnp.concatenate(parts, axis=0)
        return (mixed * g_s[r]).astype(jnp.bfloat16)

    def attend(m, g, src):
        col = lax.broadcasted_iota(jnp.int32, (W, C), 0)
        length = length_of(g)
        weights = head_weights(1)

        def live_of(r):
            return col < jnp.where(first_row + r < length, length, 0)

        def chunk(b, carry):
            gated = [row_mixed(m, g, b * RB + rr) for rr in range(RB)]
            joined = gated[0] if RB == 1 else jnp.concatenate(gated, axis=0)
            update = dot32(joined, wo_ref[m])
            done = []
            for rr in range(RB):
                r = b * RB + rr
                u = jnp.where(live_of(r), update[rr * W : (rr + 1) * W], 0.0)
                done.append((src[g, r].astype(jnp.float32) + u).astype(jnp.bfloat16))
            if m == 1:
                second = done[0] if RB == 1 else jnp.concatenate(done, axis=0)
                y = layer_norm(second, gain_ref[2:3, :], shift_ref[2:3, :])
                hidden = jnp.maximum(dot32(y, up_ref[...]), 0.0).astype(jnp.bfloat16)
                update = dot32(hidden, down_ref[...])
                for rr in range(RB):
                    r = b * RB + rr
                    u = jnp.where(live_of(r), update[rr * W : (rr + 1) * W], 0.0)
                    done[rr] = (done[rr].astype(jnp.float32) + u).astype(jnp.bfloat16)
            for rr in range(RB):
                r = b * RB + rr
                send_s[g, r] = done[rr].reshape(count, R, C)
                landed[m, g, first_row + r] = send_s[g, r, me]
            each_peer(lambda d: flip_copy(m, g, d, b * RB, RB).start())
            if m == 0:
                first = done[0] if RB == 1 else jnp.concatenate(done, axis=0)
                put_bias(weights, layer_norm(first, gain_ref[1:2, :], shift_ref[1:2, :]), b)
            return carry

        lax.fori_loop(0, R // RB, chunk, 0)

    def gather_flip(m, g, target):
        each_peer(lambda d: flip_copy(m, g, d, 0, R).wait_recv())

        def one(p, carry):
            rows = pl.ds(pl.multiple_of(p * R, R), R)
            tsc[p] = landed[m, g, rows].astype(jnp.float32)
            for c in range(R):
                target[g, c, rows, :] = tsc[p, :, c, :].astype(jnp.bfloat16)
            return carry

        lax.fori_loop(0, count, one, 0, unroll=count <= 8)

    column = lax.broadcasted_iota(jnp.int32, (R, W), 1)
    row = lax.broadcasted_iota(jnp.int32, (R, W), 0) + first_row

    def begin(g, carry):
        norm_bias(g)

        @pl.when(g == 0)
        def _():
            pl.semaphore_wait(barrier, count - 1)

        send_bias(0, g, column < length_of(g))
        return carry

    def start_node(g, carry):
        project(0, g)
        each_peer(lambda d: bias_copy(0, g, d).wait_recv())
        attend(0, g, x_ref)
        send_bias(1, g, row < length_of(g))
        return carry

    def end_node(g, carry):
        gather_flip(0, g, x1)
        project(1, g)
        each_peer(lambda d: bias_copy(1, g, d).wait_recv())
        turn_bias(g)
        each_peer(lambda d: flip_copy(0, g, d, 0, R).wait_send())
        attend(1, g, x1)
        return carry

    def finish(g, carry):
        gather_flip(1, g, out_ref)
        each_peer(lambda d: flip_copy(1, g, d, 0, R).wait_send())
        for m in range(2):
            each_peer(lambda d: bias_copy(m, g, d).wait_send())
        return carry

    for stage in (begin, start_node, end_node, finish):
        lax.fori_loop(0, G, stage, 0)


def on_device(
    pair_state, lengths, norm_gain, norm_shift, attn_proj, bias_proj, attn_out, trans_up, trans_down
):
    G, R, W, C = pair_state.shape
    count = lax.axis_size("dap")
    RB = 4 if W <= 128 else 1
    wb = jnp.swapaxes(bias_proj, 1, 2)
    bf = jnp.bfloat16
    f32 = jnp.float32
    vm = pl.BlockSpec(memory_space=pltpu.VMEM)
    return pl.pallas_call(
        partial(kernel, (count, G, R, W, C, RB)),
        out_shape=jax.ShapeDtypeStruct((G, R, W, C), bf),
        in_specs=[pl.BlockSpec(memory_space=pltpu.SMEM)] + [vm] * 8,
        out_specs=vm,
        scratch_shapes=[
            pltpu.VMEM((G, R, W, C), bf),
            pltpu.VMEM((2, G, W, R, C), bf),
            pltpu.VMEM((G, R, W, C), bf),
            pltpu.VMEM((R, W, C), bf),
            pltpu.VMEM((R, W, C), bf),
            pltpu.VMEM((R, W, C), bf),
            pltpu.VMEM((R, W, C), f32),
            pltpu.VMEM((count, R, R, C), f32),
            pltpu.VMEM((R, 8, W), f32),
            pltpu.VMEM((HEADS, W, W), bf),
            pltpu.VMEM((2, count, G, HEADS, R, W), bf),
            pltpu.VMEM((G, R, count, R, C), bf),
            pltpu.SemaphoreType.DMA((2, G, count)),
            pltpu.SemaphoreType.DMA((2, G, count)),
            pltpu.SemaphoreType.DMA((2, G, count)),
            pltpu.SemaphoreType.DMA((2, G, count)),
        ],
        compiler_params=pltpu.CompilerParams(
            collective_id=0, has_side_effects=True, vmem_limit_bytes=60 * 1024 * 1024
        ),
        name="evoformer_pair",
    )(lengths, pair_state, norm_gain, norm_shift, attn_proj, wb, attn_out, trans_up, trans_down)


def solution(mesh):
    in_specs = (P("grp", "dap", None, None), P(), P(), P(), P(), P(), P(), P(), P())
    out_specs = P("grp", "dap", None, None)
    return jax.shard_map(
        on_device, mesh=mesh, in_specs=in_specs, out_specs=out_specs, check_vma=False
    )
```

```python
from functools import partial

import jax
import jax.numpy as jnp
from jax import lax
from jax.experimental import pallas as pl
from jax.experimental.pallas import tpu as pltpu
from jax.sharding import PartitionSpec as P

HEADS = 4
HEAD_DIM = 32
EPSILON = 1e-05
MASKED = -1e30
JBLOCK = 128

NT = (((1,), (1,)), ((), ()))


def layer_norm(values, gain_row, shift_row):
    chans = values.shape[-1]
    center = values.astype(jnp.float32) - dot32(
        values, jnp.full((chans, chans), 1.0 / chans, jnp.bfloat16)
    )
    square = center * center
    high = square.astype(jnp.bfloat16)
    low = (square - high.astype(jnp.float32)).astype(jnp.bfloat16)
    spread = dot32(
        jnp.concatenate([high, low], axis=-1),
        jnp.full((2 * chans, chans), 1.0 / chans, jnp.bfloat16),
    )
    return (center * lax.rsqrt(spread + EPSILON) * gain_row + shift_row).astype(jnp.bfloat16)


def dot32(left, right):
    return jnp.dot(left, right, preferred_element_type=jnp.float32)


def kernel(
    dims,
    lens_ref,
    x_ref,
    gain_ref,
    shift_ref,
    proj_ref,
    wb_ref,
    wo_ref,
    up_ref,
    down_ref,
    out_ref,
    x1,
    landed,
    y_s,
    q_s,
    k_s,
    v_s,
    g_s,
    tsc,
    bsc,
    bias_t,
    turned_s,
    bias_s,
    send_s,
    bias_send,
    bias_recv,
    flip_send,
    flip_recv,
):
    count, G, R, W, C, RB = dims
    me = lax.axis_index("dap")
    grp = lax.axis_index("grp")
    first_row = me * R

    barrier = pltpu.get_barrier_semaphore()

    def greet(d, carry):
        pl.semaphore_signal(
            barrier,
            inc=1,
            device_id=(grp, lax.rem(me + d, count)),
            device_id_type=pl.DeviceIdType.MESH,
        )
        return carry

    lax.fori_loop(1, count, greet, 0)

    pick = lax.broadcasted_iota(jnp.int32, (8, HEADS), 0) == lax.broadcasted_iota(
        jnp.int32, (8, HEADS), 1
    )
    pick = jnp.where(pick, 1.0, 0.0).astype(jnp.bfloat16)

    def length_of(g):
        return lens_ref[grp * G + g]

    def head_weights(m):
        return dot32(pick, wb_ref[m]).astype(jnp.bfloat16)

    def put_bias(weights, y, b):
        bias = lax.dot_general(weights, y, NT, preferred_element_type=jnp.float32)
        for rr in range(RB):
            bsc[b * RB + rr] = bias[:, rr * W : (rr + 1) * W]

    def send_bias(m, g, live):
        for h in range(HEADS):
            bias_s[m, me, g, h] = jnp.where(live, bsc[:, h, :], MASKED).astype(jnp.bfloat16)
        each_peer(lambda d: bias_copy(m, g, d).start())

    def bias_copy(m, g, d):
        return pltpu.make_async_remote_copy(
            src_ref=bias_s.at[m, me, g],
            dst_ref=bias_s.at[m, me, g],
            send_sem=bias_send.at[m, g, d],
            recv_sem=bias_recv.at[m, g, d],
            device_id=(grp, lax.rem(me + d, count)),
            device_id_type=pl.DeviceIdType.MESH,
        )

    def flip_copy(m, g, d, start, size):
        peer = lax.rem(me + d, count)
        return pltpu.make_async_remote_copy(
            src_ref=send_s.at[g, pl.ds(start, size), peer],
            dst_ref=landed.at[m, g, pl.ds(first_row + start, size)],
            send_sem=flip_send.at[m, g, d],
            recv_sem=flip_recv.at[m, g, d],
            device_id=(grp, peer),
            device_id_type=pl.DeviceIdType.MESH,
        )

    def each_peer(act):
        def one(d, carry):
            act(d)
            return carry

        lax.fori_loop(1, count, one, 0, unroll=count <= 8)

    def norm_bias(g):
        weights = head_weights(0)

        def chunk(b, carry):
            rows = pl.ds(b * RB, RB)
            y = layer_norm(x_ref[g, rows].reshape(RB * W, C), gain_ref[0:1, :], shift_ref[0:1, :])
            y_s[g, rows] = y.reshape(RB, W, C)
            put_bias(weights, y, b)
            return carry

        lax.fori_loop(0, R // RB, chunk, 0)

    def project(m, g):
        def chunk(b, carry):
            rows = pl.ds(b * RB, RB)
            if m == 0:
                y = y_s[g, rows].reshape(RB * W, C)
            else:
                y = layer_norm(
                    x1[g, rows].reshape(RB * W, C), gain_ref[1:2, :], shift_ref[1:2, :]
                )
            k_s[rows] = (
                dot32(y, proj_ref[m, :, C : 2 * C]).astype(jnp.bfloat16).reshape(RB, W, C)
            )
            p = lax.dot_general(turned_s[m], y, NT, preferred_element_type=jnp.float32)
            for rr in range(RB):
                r = b * RB + rr
                at = slice(rr * W, (rr + 1) * W)
                q_s[r] = (p[:C, at] * HEAD_DIM ** (-0.5)).astype(jnp.bfloat16)
                v_s[r] = p[C : 2 * C, at].astype(jnp.bfloat16)
                g_s[r] = jax.nn.sigmoid(p[2 * C :, at])
            return carry

        lax.fori_loop(0, R // RB, chunk, 0)

    def turn_bias(g):
        per = JBLOCK // R
        for h in range(HEADS):
            for kb in range(W // JBLOCK):
                part = bias_s[0, kb * per : (kb + 1) * per, g, h].reshape(JBLOCK, W)
                bias_t[h, :, kb * JBLOCK : (kb + 1) * JBLOCK] = part.astype(jnp.float32).T.astype(
                    jnp.bfloat16
                )

    def row_gated(m, g, r):
        k = k_s[r]
        rows = []
        for jb in range(W // JBLOCK):
            at = slice(jb * JBLOCK, (jb + 1) * JBLOCK)
            q = q_s[r, :, at]
            head = lax.broadcasted_iota(jnp.int32, (C, JBLOCK), 0) // HEAD_DIM
            spread = jnp.concatenate(
                [jnp.where(head == h, q, jnp.zeros_like(q)) for h in range(HEADS)], axis=1
            )
            scores = dot32(k, spread)
            parts = []
            for h in range(HEADS):
                if m == 0:
                    bias = bias_t[h, :, at]
                else:
                    bias = bias_s[1, :, g, h, :, at].reshape(W, JBLOCK)
                s = scores[:, h * JBLOCK : (h + 1) * JBLOCK] + bias.astype(jnp.float32)
                top = jnp.max(s, 0, keepdims=True)
                weights = jnp.exp(s - top).astype(jnp.bfloat16)
                left = jnp.concatenate(
                    [
                        v_s[r, h * HEAD_DIM : (h + 1) * HEAD_DIM, :],
                        jnp.ones((16, W), jnp.bfloat16),
                    ],
                    axis=0,
                )
                summed = dot32(left, weights)
                parts.append(summed[:HEAD_DIM] / summed[HEAD_DIM : HEAD_DIM + 1])
            gated = jnp.concatenate(parts, axis=0) * g_s[r, :, at]
            rows.append(gated.T.astype(jnp.bfloat16))
        return rows[0] if len(rows) == 1 else jnp.concatenate(rows, axis=0)

    def attend(m, g, src):
        col = lax.broadcasted_iota(jnp.int32, (W, C), 0)
        length = length_of(g)
        weights = head_weights(1)

        def live_of(r):
            return col < jnp.where(first_row + r < length, length, 0)

        def chunk(b, carry):
            gated = [row_gated(m, g, b * RB + rr) for rr in range(RB)]
            joined = gated[0] if RB == 1 else jnp.concatenate(gated, axis=0)
            update = dot32(joined, wo_ref[m])
            done = []
            for rr in range(RB):
                r = b * RB + rr
                u = jnp.where(live_of(r), update[rr * W : (rr + 1) * W], 0.0)
                done.append((src[g, r].astype(jnp.float32) + u).astype(jnp.bfloat16))
            if m == 1:
                second = done[0] if RB == 1 else jnp.concatenate(done, axis=0)
                y = layer_norm(second, gain_ref[2:3, :], shift_ref[2:3, :])
                hidden = jnp.maximum(dot32(y, up_ref[...]), 0.0).astype(jnp.bfloat16)
                update = dot32(hidden, down_ref[...])
                for rr in range(RB):
                    r = b * RB + rr
                    u = jnp.where(live_of(r), update[rr * W : (rr + 1) * W], 0.0)
                    done[rr] = (done[rr].astype(jnp.float32) + u).astype(jnp.bfloat16)
            for rr in range(RB):
                r = b * RB + rr
                send_s[g, r] = done[rr].reshape(count, R, C)
                landed[m, g, first_row + r] = send_s[g, r, me]
            each_peer(lambda d: flip_copy(m, g, d, b * RB, RB).start())
            if m == 0:
                first = done[0] if RB == 1 else jnp.concatenate(done, axis=0)
                put_bias(weights, layer_norm(first, gain_ref[1:2, :], shift_ref[1:2, :]), b)
            return carry

        lax.fori_loop(0, R // RB, chunk, 0)

    def gather_flip(m, g, target):
        each_peer(lambda d: flip_copy(m, g, d, 0, R).wait_recv())

        def one(p, carry):
            rows = pl.ds(pl.multiple_of(p * R, R), R)
            tsc[p] = landed[m, g, rows].astype(jnp.float32)
            for c in range(R):
                target[g, c, rows, :] = tsc[p, :, c, :].astype(jnp.bfloat16)
            return carry

        lax.fori_loop(0, count, one, 0, unroll=count <= 8)

    column = lax.broadcasted_iota(jnp.int32, (R, W), 1)
    row = lax.broadcasted_iota(jnp.int32, (R, W), 0) + first_row

    def begin(g, carry):
        norm_bias(g)

        @pl.when(g == 0)
        def _():
            pl.semaphore_wait(barrier, count - 1)

        send_bias(0, g, column < length_of(g))
        return carry

    def start_node(g, carry):
        project(0, g)
        each_peer(lambda d: bias_copy(0, g, d).wait_recv())
        turn_bias(g)
        attend(0, g, x_ref)
        send_bias(1, g, row < length_of(g))
        return carry

    def end_node(g, carry):
        gather_flip(0, g, x1)
        project(1, g)
        each_peer(lambda d: bias_copy(1, g, d).wait_recv())
        each_peer(lambda d: flip_copy(0, g, d, 0, R).wait_send())
        attend(1, g, x1)
        return carry

    def finish(g, carry):
        gather_flip(1, g, out_ref)
        each_peer(lambda d: flip_copy(1, g, d, 0, R).wait_send())
        for m in range(2):
            each_peer(lambda d: bias_copy(m, g, d).wait_send())
        return carry

    for m in range(2):
        for at, first in enumerate((0, 2 * C, 3 * C)):
            part = proj_ref[m, :, first : first + C].astype(jnp.float32)
            turned_s[m, at * C : (at + 1) * C, :] = part.T.astype(jnp.bfloat16)
    for stage in (begin, start_node, end_node, finish):
        lax.fori_loop(0, G, stage, 0)


def on_device(
    pair_state, lengths, norm_gain, norm_shift, attn_proj, bias_proj, attn_out, trans_up, trans_down
):
    G, R, W, C = pair_state.shape
    count = lax.axis_size("dap")
    RB = 4 if W <= 128 else 1
    wb = jnp.swapaxes(bias_proj, 1, 2)
    bf = jnp.bfloat16
    f32 = jnp.float32
    vm = pl.BlockSpec(memory_space=pltpu.VMEM)
    return pl.pallas_call(
        partial(kernel, (count, G, R, W, C, RB)),
        out_shape=jax.ShapeDtypeStruct((G, R, W, C), bf),
        in_specs=[pl.BlockSpec(memory_space=pltpu.SMEM)] + [vm] * 8,
        out_specs=vm,
        scratch_shapes=[
            pltpu.VMEM((G, R, W, C), bf),
            pltpu.VMEM((2, G, W, R, C), bf),
            pltpu.VMEM((G, R, W, C), bf),
            pltpu.VMEM((R, C, W), bf),
            pltpu.VMEM((R, W, C), bf),
            pltpu.VMEM((R, C, W), bf),
            pltpu.VMEM((R, C, W), f32),
            pltpu.VMEM((count, R, R, C), f32),
            pltpu.VMEM((R, 8, W), f32),
            pltpu.VMEM((HEADS, W, W), bf),
            pltpu.VMEM((2, 3 * C, C), bf),
            pltpu.VMEM((2, count, G, HEADS, R, W), bf),
            pltpu.VMEM((G, R, count, R, C), bf),
            pltpu.SemaphoreType.DMA((2, G, count)),
            pltpu.SemaphoreType.DMA((2, G, count)),
            pltpu.SemaphoreType.DMA((2, G, count)),
            pltpu.SemaphoreType.DMA((2, G, count)),
        ],
        compiler_params=pltpu.CompilerParams(
            collective_id=0, has_side_effects=True, vmem_limit_bytes=60 * 1024 * 1024
        ),
        name="evoformer_pair",
    )(lengths, pair_state, norm_gain, norm_shift, attn_proj, wb, attn_out, trans_up, trans_down)


def solution(mesh):
    in_specs = (P("grp", "dap", None, None), P(), P(), P(), P(), P(), P(), P(), P())
    out_specs = P("grp", "dap", None, None)
    return jax.shard_map(
        on_device, mesh=mesh, in_specs=in_specs, out_specs=out_specs, check_vma=False
    )
```

```python
from functools import partial

import jax
import jax.numpy as jnp
from jax import lax
from jax.experimental import pallas as pl
from jax.experimental.pallas import tpu as pltpu
from jax.sharding import PartitionSpec as P

HEADS = 4
HEAD_DIM = 32
EPSILON = 1e-05
MASKED = -1e30
JBLOCK = 128

NT = (((1,), (1,)), ((), ()))


def layer_norm(values, gain_row, shift_row):
    chans = values.shape[-1]
    center = values.astype(jnp.float32) - dot32(
        values, jnp.full((chans, chans), 1.0 / chans, jnp.bfloat16)
    )
    square = center * center
    high = square.astype(jnp.bfloat16)
    low = (square - high.astype(jnp.float32)).astype(jnp.bfloat16)
    spread = dot32(
        jnp.concatenate([high, low], axis=-1),
        jnp.full((2 * chans, chans), 1.0 / chans, jnp.bfloat16),
    )
    return (center * lax.rsqrt(spread + EPSILON) * gain_row + shift_row).astype(jnp.bfloat16)


def dot32(left, right):
    return jnp.dot(left, right, preferred_element_type=jnp.float32)


def kernel(
    dims,
    lens_ref,
    x_ref,
    gain_ref,
    shift_ref,
    proj_ref,
    wb_ref,
    wo_ref,
    up_ref,
    down_ref,
    out_ref,
    x1,
    landed,
    y_s,
    q_s,
    k_s,
    v_s,
    g_s,
    tsc,
    bsc,
    bias_t,
    turned_s,
    bias_s,
    send_s,
    bias_send,
    bias_recv,
    flip_send,
    flip_recv,
):
    count, G, R, W, C, RB = dims
    me = lax.axis_index("dap")
    grp = lax.axis_index("grp")
    first_row = me * R

    barrier = pltpu.get_barrier_semaphore()

    def greet(d, carry):
        pl.semaphore_signal(
            barrier,
            inc=1,
            device_id=(grp, lax.rem(me + d, count)),
            device_id_type=pl.DeviceIdType.MESH,
        )
        return carry

    lax.fori_loop(1, count, greet, 0)

    pick = lax.broadcasted_iota(jnp.int32, (8, HEADS), 0) == lax.broadcasted_iota(
        jnp.int32, (8, HEADS), 1
    )
    pick = jnp.where(pick, 1.0, 0.0).astype(jnp.bfloat16)

    def length_of(g):
        return lens_ref[grp * G + g]

    def head_weights(m):
        return dot32(pick, wb_ref[m]).astype(jnp.bfloat16)

    def put_bias(weights, y, b):
        bias = lax.dot_general(weights, y, NT, preferred_element_type=jnp.float32)
        for rr in range(RB):
            bsc[b * RB + rr] = bias[:, rr * W : (rr + 1) * W]

    def send_bias(m, g, live):
        for h in range(HEADS):
            bias_s[m, me, g, h] = jnp.where(live, bsc[:, h, :], MASKED).astype(jnp.bfloat16)
        bias_copy(m, g, 0, True).start()
        each_chip(1, lambda e: bias_copy(m, g, e, False).start())

    sibling = me + 1 - 2 * lax.rem(me, 2)

    def bias_copy(m, g, e, relay):
        block = lax.rem(me - 2 * e + count, count) if relay else me
        peer = sibling if relay else lax.rem(me + 2 * e, count)
        place = 2 * e + 1 if relay else 2 * e
        return pltpu.make_async_remote_copy(
            src_ref=bias_s.at[m, block, g],
            dst_ref=bias_s.at[m, block, g],
            send_sem=bias_send.at[m, g, place],
            recv_sem=bias_recv.at[m, g, place],
            device_id=(grp, peer),
            device_id_type=pl.DeviceIdType.MESH,
        )

    def each_chip(first, act):
        def one(e, carry):
            act(e)
            return carry

        lax.fori_loop(first, count // 2, one, 0, unroll=count <= 8)

    def relay_bias(m, g):
        def one(e):
            bias_copy(m, g, e, False).wait_recv()
            bias_copy(m, g, e, True).start()

        each_chip(1, one)

    def flip_copy(m, g, d, start, size):
        peer = lax.rem(me + d, count)
        return pltpu.make_async_remote_copy(
            src_ref=send_s.at[g, peer, pl.ds(start, size)],
            dst_ref=landed.at[m, g, pl.ds(first_row + start, size)],
            send_sem=flip_send.at[m, g, d],
            recv_sem=flip_recv.at[m, g, d],
            device_id=(grp, peer),
            device_id_type=pl.DeviceIdType.MESH,
        )

    def each_peer(act):
        if count <= 8:
            for d in sorted(range(1, count), key=lambda d: abs(2 * d - count)):
                act(d)
            return

        def one(d, carry):
            act(d)
            return carry

        lax.fori_loop(1, count, one, 0)

    def norm_bias(g):
        weights = head_weights(0)

        def chunk(b, carry):
            rows = pl.ds(b * RB, RB)
            y = layer_norm(x_ref[g, rows].reshape(RB * W, C), gain_ref[0:1, :], shift_ref[0:1, :])
            y_s[g, rows] = y.reshape(RB, W, C)
            put_bias(weights, y, b)
            return carry

        lax.fori_loop(0, R // RB, chunk, 0)

    def project(m, g):
        def chunk(b, carry):
            rows = pl.ds(b * RB, RB)
            if m == 0:
                y = y_s[g, rows].reshape(RB * W, C)
            else:
                y = layer_norm(
                    x1[g, rows].reshape(RB * W, C), gain_ref[1:2, :], shift_ref[1:2, :]
                )
            k_s[rows] = (
                dot32(y, proj_ref[m, :, C : 2 * C]).astype(jnp.bfloat16).reshape(RB, W, C)
            )
            p = lax.dot_general(turned_s[m], y, NT, preferred_element_type=jnp.float32)
            for rr in range(RB):
                r = b * RB + rr
                at = slice(rr * W, (rr + 1) * W)
                q_s[r] = (p[:C, at] * HEAD_DIM ** (-0.5)).astype(jnp.bfloat16)
                v_s[r] = p[C : 2 * C, at].astype(jnp.bfloat16)
                g_s[r] = jax.nn.sigmoid(p[2 * C :, at])
            return carry

        lax.fori_loop(0, R // RB, chunk, 0)

    def turn_bias(g):
        per = JBLOCK // R
        for h in range(HEADS):
            for kb in range(W // JBLOCK):
                part = bias_s[0, kb * per : (kb + 1) * per, g, h].reshape(JBLOCK, W)
                bias_t[h, :, kb * JBLOCK : (kb + 1) * JBLOCK] = part.astype(jnp.float32).T.astype(
                    jnp.bfloat16
                )

    def row_gated(m, g, r):
        k = k_s[r]
        rows = []
        for jb in range(W // JBLOCK):
            at = slice(jb * JBLOCK, (jb + 1) * JBLOCK)
            q = q_s[r, :, at]
            head = lax.broadcasted_iota(jnp.int32, (C, JBLOCK), 0) // HEAD_DIM
            spread = jnp.concatenate(
                [jnp.where(head == h, q, jnp.zeros_like(q)) for h in range(HEADS)], axis=1
            )
            scores = dot32(k, spread)
            parts = []
            for h in range(HEADS):
                if m == 0:
                    bias = bias_t[h, :, at]
                else:
                    bias = bias_s[1, :, g, h, :, at].reshape(W, JBLOCK)
                s = scores[:, h * JBLOCK : (h + 1) * JBLOCK] + bias.astype(jnp.float32)
                top = jnp.max(s, 0, keepdims=True)
                weights = jnp.exp(s - top).astype(jnp.bfloat16)
                left = jnp.concatenate(
                    [
                        v_s[r, h * HEAD_DIM : (h + 1) * HEAD_DIM, :],
                        jnp.ones((16, W), jnp.bfloat16),
                    ],
                    axis=0,
                )
                summed = dot32(left, weights)
                parts.append(summed[:HEAD_DIM] / summed[HEAD_DIM : HEAD_DIM + 1])
            gated = jnp.concatenate(parts, axis=0) * g_s[r, :, at]
            rows.append(gated.T.astype(jnp.bfloat16))
        return rows[0] if len(rows) == 1 else jnp.concatenate(rows, axis=0)

    def attend(m, g, src):
        col = lax.broadcasted_iota(jnp.int32, (W, C), 0)
        length = length_of(g)
        weights = head_weights(1)

        def live_of(r):
            return col < jnp.where(first_row + r < length, length, 0)

        def chunk(b, carry):
            gated = [row_gated(m, g, b * RB + rr) for rr in range(RB)]
            joined = gated[0] if RB == 1 else jnp.concatenate(gated, axis=0)
            update = dot32(joined, wo_ref[m])
            done = []
            for rr in range(RB):
                r = b * RB + rr
                u = jnp.where(live_of(r), update[rr * W : (rr + 1) * W], 0.0)
                done.append((src[g, r].astype(jnp.float32) + u).astype(jnp.bfloat16))
            if m == 1:
                second = done[0] if RB == 1 else jnp.concatenate(done, axis=0)
                y = layer_norm(second, gain_ref[2:3, :], shift_ref[2:3, :])
                hidden = jnp.maximum(dot32(y, up_ref[...]), 0.0).astype(jnp.bfloat16)
                update = dot32(hidden, down_ref[...])
                for rr in range(RB):
                    r = b * RB + rr
                    u = jnp.where(live_of(r), update[rr * W : (rr + 1) * W], 0.0)
                    done[rr] = (done[rr].astype(jnp.float32) + u).astype(jnp.bfloat16)
            for rr in range(RB):
                r = b * RB + rr
                send_s[g, :, r] = done[rr].reshape(count, R, C)
                landed[m, g, first_row + r] = send_s[g, me, r]
            each_peer(lambda d: flip_copy(m, g, d, b * RB, RB).start())
            if m == 0:
                first = done[0] if RB == 1 else jnp.concatenate(done, axis=0)
                put_bias(weights, layer_norm(first, gain_ref[1:2, :], shift_ref[1:2, :]), b)
            return carry

        lax.fori_loop(0, R // RB, chunk, 0)

    def gather_flip(m, g, target):
        each_peer(lambda d: flip_copy(m, g, d, 0, R).wait_recv())

        def one(p, carry):
            rows = pl.ds(pl.multiple_of(p * R, R), R)
            tsc[p] = landed[m, g, rows].astype(jnp.float32)
            for c in range(R):
                target[g, c, rows, :] = tsc[p, :, c, :].astype(jnp.bfloat16)
            return carry

        lax.fori_loop(0, count, one, 0, unroll=count <= 8)

    column = lax.broadcasted_iota(jnp.int32, (R, W), 1)
    row = lax.broadcasted_iota(jnp.int32, (R, W), 0) + first_row

    def begin(g, carry):
        norm_bias(g)

        @pl.when(g == 0)
        def _():
            pl.semaphore_wait(barrier, count - 1)

        send_bias(0, g, column < length_of(g))
        return carry

    def start_node(g, carry):
        relay_bias(0, g)
        project(0, g)
        each_chip(0, lambda e: bias_copy(0, g, e, True).wait_recv())
        turn_bias(g)
        attend(0, g, x_ref)
        send_bias(1, g, row < length_of(g))
        return carry

    def end_node(g, carry):
        relay_bias(1, g)
        gather_flip(0, g, x1)
        project(1, g)
        each_chip(0, lambda e: bias_copy(1, g, e, True).wait_recv())
        each_peer(lambda d: flip_copy(0, g, d, 0, R).wait_send())
        attend(1, g, x1)
        return carry

    def finish(g, carry):
        gather_flip(1, g, out_ref)
        each_peer(lambda d: flip_copy(1, g, d, 0, R).wait_send())
        for m in range(2):
            each_chip(0, lambda e: bias_copy(m, g, e, True).wait_send())
            each_chip(1, lambda e: bias_copy(m, g, e, False).wait_send())
        return carry

    for m in range(2):
        for at, first in enumerate((0, 2 * C, 3 * C)):
            part = proj_ref[m, :, first : first + C].astype(jnp.float32)
            turned_s[m, at * C : (at + 1) * C, :] = part.T.astype(jnp.bfloat16)
    for stage in (begin, start_node, end_node, finish):
        lax.fori_loop(0, G, stage, 0)


def on_device(
    pair_state, lengths, norm_gain, norm_shift, attn_proj, bias_proj, attn_out, trans_up, trans_down
):
    G, R, W, C = pair_state.shape
    count = lax.axis_size("dap")
    RB = 4 if W <= 128 else 1
    wb = jnp.swapaxes(bias_proj, 1, 2)
    bf = jnp.bfloat16
    f32 = jnp.float32
    vm = pl.BlockSpec(memory_space=pltpu.VMEM)
    return pl.pallas_call(
        partial(kernel, (count, G, R, W, C, RB)),
        out_shape=jax.ShapeDtypeStruct((G, R, W, C), bf),
        in_specs=[pl.BlockSpec(memory_space=pltpu.SMEM)] + [vm] * 8,
        out_specs=vm,
        scratch_shapes=[
            pltpu.VMEM((G, R, W, C), bf),
            pltpu.VMEM((2, G, W, R, C), bf),
            pltpu.VMEM((G, R, W, C), bf),
            pltpu.VMEM((R, C, W), bf),
            pltpu.VMEM((R, W, C), bf),
            pltpu.VMEM((R, C, W), bf),
            pltpu.VMEM((R, C, W), f32),
            pltpu.VMEM((count, R, R, C), f32),
            pltpu.VMEM((R, 8, W), f32),
            pltpu.VMEM((HEADS, W, W), bf),
            pltpu.VMEM((2, 3 * C, C), bf),
            pltpu.VMEM((2, count, G, HEADS, R, W), bf),
            pltpu.VMEM((G, count, R, R, C), bf),
            pltpu.SemaphoreType.DMA((2, G, count)),
            pltpu.SemaphoreType.DMA((2, G, count)),
            pltpu.SemaphoreType.DMA((2, G, count)),
            pltpu.SemaphoreType.DMA((2, G, count)),
        ],
        compiler_params=pltpu.CompilerParams(
            collective_id=0, has_side_effects=True, vmem_limit_bytes=60 * 1024 * 1024
        ),
        name="evoformer_pair",
    )(lengths, pair_state, norm_gain, norm_shift, attn_proj, wb, attn_out, trans_up, trans_down)


def solution(mesh):
    in_specs = (P("grp", "dap", None, None), P(), P(), P(), P(), P(), P(), P(), P())
    out_specs = P("grp", "dap", None, None)
    return jax.shard_map(
        on_device, mesh=mesh, in_specs=in_specs, out_specs=out_specs, check_vma=False
    )
```

```python
from functools import partial

import jax
import jax.numpy as jnp
from jax import lax
from jax.experimental import pallas as pl
from jax.experimental.pallas import tpu as pltpu
from jax.sharding import PartitionSpec as P

HEADS = 4
HEAD_DIM = 32
EPSILON = 1e-05
MASKED = -1e30
JBLOCK = 128

NT = (((1,), (1,)), ((), ()))


def layer_norm(values, gain_row, shift_row):
    chans = values.shape[-1]
    center = values.astype(jnp.float32) - dot32(
        values, jnp.full((chans, chans), 1.0 / chans, jnp.bfloat16)
    )
    square = center * center
    high = square.astype(jnp.bfloat16)
    low = (square - high.astype(jnp.float32)).astype(jnp.bfloat16)
    spread = dot32(
        jnp.concatenate([high, low], axis=-1),
        jnp.full((2 * chans, chans), 1.0 / chans, jnp.bfloat16),
    )
    return (center * lax.rsqrt(spread + EPSILON) * gain_row + shift_row).astype(jnp.bfloat16)


def dot32(left, right):
    return jnp.dot(left, right, preferred_element_type=jnp.float32)


def kernel(
    dims,
    lens_ref,
    x_ref,
    gain_ref,
    shift_ref,
    proj_ref,
    wb_ref,
    wo_ref,
    up_ref,
    down_ref,
    out_ref,
    x1,
    landed,
    y_s,
    q_s,
    k_s,
    v_s,
    g_s,
    tsc,
    bsc,
    bias_t,
    turned_s,
    bias_s,
    send_s,
    bias_send,
    bias_recv,
    flip_send,
    flip_recv,
):
    count, G, R, W, C, RB = dims
    me = lax.axis_index("dap")
    grp = lax.axis_index("grp")
    first_row = me * R

    barrier = pltpu.get_barrier_semaphore()

    def greet(d, carry):
        pl.semaphore_signal(
            barrier,
            inc=1,
            device_id=(grp, lax.rem(me + d, count)),
            device_id_type=pl.DeviceIdType.MESH,
        )
        return carry

    lax.fori_loop(1, count, greet, 0)

    pick = lax.broadcasted_iota(jnp.int32, (8, HEADS), 0) == lax.broadcasted_iota(
        jnp.int32, (8, HEADS), 1
    )
    pick = jnp.where(pick, 1.0, 0.0).astype(jnp.bfloat16)

    def length_of(g):
        return lens_ref[grp * G + g]

    def head_weights(m):
        return dot32(pick, wb_ref[m]).astype(jnp.bfloat16)

    def put_bias(weights, y, b):
        bias = lax.dot_general(weights, y, NT, preferred_element_type=jnp.float32)
        for rr in range(RB):
            bsc[b * RB + rr] = bias[:, rr * W : (rr + 1) * W]

    def send_bias(m, g, live):
        for h in range(HEADS):
            bias_s[m, me, g, h] = jnp.where(live, bsc[:, h, :], MASKED).astype(jnp.bfloat16)
        bias_copy(m, g, 0, True).start()
        each_chip(1, lambda e: bias_copy(m, g, e, False).start())

    sibling = me + 1 - 2 * lax.rem(me, 2)

    def bias_copy(m, g, e, relay):
        block = lax.rem(me - 2 * e + count, count) if relay else me
        peer = sibling if relay else lax.rem(me + 2 * e, count)
        place = 2 * e + 1 if relay else 2 * e
        return pltpu.make_async_remote_copy(
            src_ref=bias_s.at[m, block, g],
            dst_ref=bias_s.at[m, block, g],
            send_sem=bias_send.at[m, g, place],
            recv_sem=bias_recv.at[m, g, place],
            device_id=(grp, peer),
            device_id_type=pl.DeviceIdType.MESH,
        )

    def each_chip(first, act):
        def one(e, carry):
            act(e)
            return carry

        lax.fori_loop(first, count // 2, one, 0, unroll=count <= 8)

    def relay_bias(m, g):
        def one(e):
            bias_copy(m, g, e, False).wait_recv()
            bias_copy(m, g, e, True).start()

        each_chip(1, one)

    def flip_copy(m, g, d, start, size):
        peer = lax.rem(me + d, count)
        return pltpu.make_async_remote_copy(
            src_ref=send_s.at[g, peer, pl.ds(start, size)],
            dst_ref=landed.at[m, g, pl.ds(first_row + start, size)],
            send_sem=flip_send.at[m, g, d],
            recv_sem=flip_recv.at[m, g, d],
            device_id=(grp, peer),
            device_id_type=pl.DeviceIdType.MESH,
        )

    def each_peer(act):
        if count <= 8:
            for d in sorted(range(1, count), key=lambda d: abs(2 * d - count)):
                act(d)
            return

        def one(d, carry):
            act(d)
            return carry

        lax.fori_loop(1, count, one, 0)

    def norm_bias(g):
        weights = head_weights(0)

        def chunk(b, carry):
            rows = pl.ds(b * RB, RB)
            y = layer_norm(x_ref[g, rows].reshape(RB * W, C), gain_ref[0:1, :], shift_ref[0:1, :])
            y_s[g, rows] = y.reshape(RB, W, C)
            put_bias(weights, y, b)
            return carry

        lax.fori_loop(0, R // RB, chunk, 0)

    def project(m, g):
        def chunk(b, carry):
            rows = pl.ds(b * RB, RB)
            if m == 0:
                y = y_s[g, rows].reshape(RB * W, C)
            else:
                y = layer_norm(
                    x1[g, rows].reshape(RB * W, C), gain_ref[1:2, :], shift_ref[1:2, :]
                )
            k_s[rows] = (
                dot32(y, proj_ref[m, :, C : 2 * C]).astype(jnp.bfloat16).reshape(RB, W, C)
            )
            p = lax.dot_general(turned_s[m], y, NT, preferred_element_type=jnp.float32)
            for rr in range(RB):
                r = b * RB + rr
                at = slice(rr * W, (rr + 1) * W)
                q_s[r] = (p[:C, at] * HEAD_DIM ** (-0.5)).astype(jnp.bfloat16)
                v_s[r] = p[C : 2 * C, at].astype(jnp.bfloat16)
                g_s[r] = jax.nn.sigmoid(p[2 * C :, at])
            return carry

        lax.fori_loop(0, R // RB, chunk, 0)

    def turn_bias(g):
        per = JBLOCK // R
        for h in range(HEADS):
            for kb in range(W // JBLOCK):
                part = bias_s[0, kb * per : (kb + 1) * per, g, h].reshape(JBLOCK, W)
                bias_t[h, :, kb * JBLOCK : (kb + 1) * JBLOCK] = part.astype(jnp.float32).T.astype(
                    jnp.bfloat16
                )

    def row_gated(m, g, r):
        k = k_s[r]
        rows = []
        for jb in range(W // JBLOCK):
            at = slice(jb * JBLOCK, (jb + 1) * JBLOCK)
            q = q_s[r, :, at]
            head = lax.broadcasted_iota(jnp.int32, (C, JBLOCK), 0) // HEAD_DIM
            spread = jnp.concatenate(
                [jnp.where(head == h, q, jnp.zeros_like(q)) for h in range(HEADS)], axis=1
            )
            scores = dot32(k, spread)
            parts = []
            for h in range(HEADS):
                if m == 0:
                    bias = bias_t[h, :, at]
                else:
                    bias = bias_s[1, :, g, h, :, at].reshape(W, JBLOCK)
                s = scores[:, h * JBLOCK : (h + 1) * JBLOCK] + bias.astype(jnp.float32)
                top = jnp.max(s, 0, keepdims=True)
                weights = jnp.exp(s - top).astype(jnp.bfloat16)
                left = jnp.concatenate(
                    [
                        v_s[r, h * HEAD_DIM : (h + 1) * HEAD_DIM, :],
                        jnp.ones((16, W), jnp.bfloat16),
                    ],
                    axis=0,
                )
                summed = dot32(left, weights)
                parts.append(summed[:HEAD_DIM] / summed[HEAD_DIM : HEAD_DIM + 1])
            gated = jnp.concatenate(parts, axis=0) * g_s[r, :, at]
            rows.append(gated.T.astype(jnp.bfloat16))
        return rows[0] if len(rows) == 1 else jnp.concatenate(rows, axis=0)

    def attend(m, g, src):
        col = lax.broadcasted_iota(jnp.int32, (W, C), 0)
        length = length_of(g)
        weights = head_weights(1)

        def live_of(r):
            return col < jnp.where(first_row + r < length, length, 0)

        def chunk(b, carry):
            gated = [row_gated(m, g, b * RB + rr) for rr in range(RB)]
            joined = gated[0] if RB == 1 else jnp.concatenate(gated, axis=0)
            update = dot32(joined, wo_ref[m])
            done = []
            for rr in range(RB):
                r = b * RB + rr
                u = jnp.where(live_of(r), update[rr * W : (rr + 1) * W], 0.0)
                done.append((src[g, r].astype(jnp.float32) + u).astype(jnp.bfloat16))
            if m == 1:
                second = done[0] if RB == 1 else jnp.concatenate(done, axis=0)
                y = layer_norm(second, gain_ref[2:3, :], shift_ref[2:3, :])
                hidden = jnp.maximum(dot32(y, up_ref[...]), 0.0).astype(jnp.bfloat16)
                update = dot32(hidden, down_ref[...])
                for rr in range(RB):
                    r = b * RB + rr
                    u = jnp.where(live_of(r), update[rr * W : (rr + 1) * W], 0.0)
                    done[rr] = (done[rr].astype(jnp.float32) + u).astype(jnp.bfloat16)
            for rr in range(RB):
                r = b * RB + rr
                send_s[g, :, r] = done[rr].reshape(count, R, C)
                landed[m, g, first_row + r] = send_s[g, me, r]
            each_peer(lambda d: flip_copy(m, g, d, b * RB, RB).start())
            if m == 0:
                first = done[0] if RB == 1 else jnp.concatenate(done, axis=0)
                put_bias(weights, layer_norm(first, gain_ref[1:2, :], shift_ref[1:2, :]), b)
            return carry

        lax.fori_loop(0, R // RB, chunk, 0)

    def gather_flip(m, g, target):
        each_peer(lambda d: flip_copy(m, g, d, 0, R).wait_recv())

        def one(p, carry):
            rows = pl.ds(pl.multiple_of(p * R, R), R)
            tsc[p] = landed[m, g, rows].astype(jnp.float32)
            for c in range(R):
                target[g, c, rows, :] = tsc[p, :, c, :].astype(jnp.bfloat16)
            return carry

        lax.fori_loop(0, count, one, 0, unroll=count <= 8)

    column = lax.broadcasted_iota(jnp.int32, (R, W), 1)
    row = lax.broadcasted_iota(jnp.int32, (R, W), 0) + first_row

    def begin(g, carry):
        norm_bias(g)

        @pl.when(g == 0)
        def _():
            pl.semaphore_wait(barrier, count - 1)

        send_bias(0, g, column < length_of(g))
        return carry

    def start_node(g, carry):
        relay_bias(0, g)
        project(0, g)
        each_chip(0, lambda e: bias_copy(0, g, e, True).wait_recv())
        turn_bias(g)
        attend(0, g, x_ref)
        send_bias(1, g, row < length_of(g))
        return carry

    def end_node(g, carry):
        relay_bias(1, g)
        gather_flip(0, g, x1)
        project(1, g)
        each_chip(0, lambda e: bias_copy(1, g, e, True).wait_recv())
        each_peer(lambda d: flip_copy(0, g, d, 0, R).wait_send())
        attend(1, g, x1)
        return carry

    def finish(g, carry):
        gather_flip(1, g, out_ref)
        each_peer(lambda d: flip_copy(1, g, d, 0, R).wait_send())
        for m in range(2):
            each_chip(0, lambda e: bias_copy(m, g, e, True).wait_send())
            each_chip(1, lambda e: bias_copy(m, g, e, False).wait_send())
        return carry

    for m in range(2):
        for at, first in enumerate((0, 2 * C, 3 * C)):
            part = proj_ref[m, :, first : first + C].astype(jnp.float32)
            turned_s[m, at * C : (at + 1) * C, :] = part.T.astype(jnp.bfloat16)
    for stage in (begin, start_node, end_node, finish):
        lax.fori_loop(0, G, stage, 0)


def on_device(
    pair_state, lengths, norm_gain, norm_shift, attn_proj, bias_proj, attn_out, trans_up, trans_down
):
    G, R, W, C = pair_state.shape
    count = lax.axis_size("dap")
    RB = 2 if W <= 128 else 1
    wb = jnp.swapaxes(bias_proj, 1, 2)
    bf = jnp.bfloat16
    f32 = jnp.float32
    vm = pl.BlockSpec(memory_space=pltpu.VMEM)
    return pl.pallas_call(
        partial(kernel, (count, G, R, W, C, RB)),
        out_shape=jax.ShapeDtypeStruct((G, R, W, C), bf),
        in_specs=[pl.BlockSpec(memory_space=pltpu.SMEM)] + [vm] * 8,
        out_specs=vm,
        scratch_shapes=[
            pltpu.VMEM((G, R, W, C), bf),
            pltpu.VMEM((2, G, W, R, C), bf),
            pltpu.VMEM((G, R, W, C), bf),
            pltpu.VMEM((R, C, W), bf),
            pltpu.VMEM((R, W, C), bf),
            pltpu.VMEM((R, C, W), bf),
            pltpu.VMEM((R, C, W), f32),
            pltpu.VMEM((count, R, R, C), f32),
            pltpu.VMEM((R, 8, W), f32),
            pltpu.VMEM((HEADS, W, W), bf),
            pltpu.VMEM((2, 3 * C, C), bf),
            pltpu.VMEM((2, count, G, HEADS, R, W), bf),
            pltpu.VMEM((G, count, R, R, C), bf),
            pltpu.SemaphoreType.DMA((2, G, count)),
            pltpu.SemaphoreType.DMA((2, G, count)),
            pltpu.SemaphoreType.DMA((2, G, count)),
            pltpu.SemaphoreType.DMA((2, G, count)),
        ],
        compiler_params=pltpu.CompilerParams(
            collective_id=0, has_side_effects=True, vmem_limit_bytes=60 * 1024 * 1024
        ),
        name="evoformer_pair",
    )(lengths, pair_state, norm_gain, norm_shift, attn_proj, wb, attn_out, trans_up, trans_down)


def solution(mesh):
    in_specs = (P("grp", "dap", None, None), P(), P(), P(), P(), P(), P(), P(), P())
    out_specs = P("grp", "dap", None, None)
    return jax.shard_map(
        on_device, mesh=mesh, in_specs=in_specs, out_specs=out_specs, check_vma=False
    )
```

```python
from functools import partial

import jax
import jax.numpy as jnp
from jax import lax
from jax.experimental import pallas as pl
from jax.experimental.pallas import tpu as pltpu
from jax.sharding import PartitionSpec as P

HEADS = 4
HEAD_DIM = 32
EPSILON = 1e-05
MASKED = -1e30
JBLOCK = 128

NT = (((1,), (1,)), ((), ()))


def layer_norm(values, gain_row, shift_row):
    chans = values.shape[-1]
    center = values.astype(jnp.float32) - dot32(
        values, jnp.full((chans, chans), 1.0 / chans, jnp.bfloat16)
    )
    square = center * center
    high = square.astype(jnp.bfloat16)
    low = (square - high.astype(jnp.float32)).astype(jnp.bfloat16)
    spread = dot32(
        jnp.concatenate([high, low], axis=-1),
        jnp.full((2 * chans, chans), 1.0 / chans, jnp.bfloat16),
    )
    return (center * lax.rsqrt(spread + EPSILON) * gain_row + shift_row).astype(jnp.bfloat16)


def dot32(left, right):
    return jnp.dot(left, right, preferred_element_type=jnp.float32)


def kernel(
    dims,
    lens_ref,
    x_ref,
    gain_ref,
    shift_ref,
    proj_ref,
    wb_ref,
    wo_ref,
    up_ref,
    down_ref,
    out_ref,
    x1,
    landed,
    y_s,
    q_s,
    k_s,
    v_s,
    g_s,
    tsc,
    bsc,
    bias_t,
    turned_s,
    bias_s,
    send_s,
    bias_send,
    bias_recv,
    flip_send,
    flip_recv,
):
    count, G, R, W, C, RB = dims
    me = lax.axis_index("dap")
    grp = lax.axis_index("grp")
    first_row = me * R

    barrier = pltpu.get_barrier_semaphore()

    def greet(d, carry):
        pl.semaphore_signal(
            barrier,
            inc=1,
            device_id=(grp, lax.rem(me + d, count)),
            device_id_type=pl.DeviceIdType.MESH,
        )
        return carry

    lax.fori_loop(1, count, greet, 0)

    pick = lax.broadcasted_iota(jnp.int32, (8, HEADS), 0) == lax.broadcasted_iota(
        jnp.int32, (8, HEADS), 1
    )
    pick = jnp.where(pick, 1.0, 0.0).astype(jnp.bfloat16)

    def length_of(g):
        return lens_ref[grp * G + g]

    def head_weights(m):
        return dot32(pick, wb_ref[m]).astype(jnp.bfloat16)

    def put_bias(weights, y, b):
        bias = lax.dot_general(weights, y, NT, preferred_element_type=jnp.float32)
        for rr in range(RB):
            bsc[b * RB + rr] = bias[:, rr * W : (rr + 1) * W]

    def send_bias(m, g, live):
        for h in range(HEADS):
            bias_s[m, me, g, h] = jnp.where(live, bsc[:, h, :], MASKED).astype(jnp.bfloat16)
        bias_copy(m, g, 0, True).start()
        each_chip(1, lambda e: bias_copy(m, g, e, False).start())

    sibling = me + 1 - 2 * lax.rem(me, 2)

    def bias_copy(m, g, e, relay):
        block = lax.rem(me - 2 * e + count, count) if relay else me
        peer = sibling if relay else lax.rem(me + 2 * e, count)
        place = 2 * e + 1 if relay else 2 * e
        return pltpu.make_async_remote_copy(
            src_ref=bias_s.at[m, block, g],
            dst_ref=bias_s.at[m, block, g],
            send_sem=bias_send.at[m, g, place],
            recv_sem=bias_recv.at[m, g, place],
            device_id=(grp, peer),
            device_id_type=pl.DeviceIdType.MESH,
        )

    def each_chip(first, act):
        def one(e, carry):
            act(e)
            return carry

        lax.fori_loop(first, count // 2, one, 0, unroll=count <= 8)

    def relay_bias(m, g):
        def one(e):
            bias_copy(m, g, e, False).wait_recv()
            bias_copy(m, g, e, True).start()

        each_chip(1, one)

    def flip_copy(m, g, d, start, size):
        peer = lax.rem(me + d, count)
        return pltpu.make_async_remote_copy(
            src_ref=send_s.at[g, peer, pl.ds(start, size)],
            dst_ref=landed.at[m, g, pl.ds(first_row + start, size)],
            send_sem=flip_send.at[m, g, d],
            recv_sem=flip_recv.at[m, g, d],
            device_id=(grp, peer),
            device_id_type=pl.DeviceIdType.MESH,
        )

    def each_peer(act):
        if count <= 8:
            for d in sorted(range(1, count), key=lambda d: abs(2 * d - count)):
                act(d)
            return

        def one(d, carry):
            act(d)
            return carry

        lax.fori_loop(1, count, one, 0)

    def norm_bias(g):
        weights = head_weights(0)

        def chunk(b, carry):
            rows = pl.ds(b * RB, RB)
            y = layer_norm(x_ref[g, rows].reshape(RB * W, C), gain_ref[0:1, :], shift_ref[0:1, :])
            y_s[g, rows] = y.reshape(RB, W, C)
            put_bias(weights, y, b)
            return carry

        lax.fori_loop(0, R // RB, chunk, 0)

    def project(m, g):
        def chunk(b, carry):
            rows = pl.ds(b * RB, RB)
            if m == 0:
                y = y_s[g, rows].reshape(RB * W, C)
            else:
                y = layer_norm(
                    x1[g, rows].reshape(RB * W, C), gain_ref[1:2, :], shift_ref[1:2, :]
                )
            k_s[rows] = (
                dot32(y, proj_ref[m, :, C : 2 * C]).astype(jnp.bfloat16).reshape(RB, W, C)
            )
            p = lax.dot_general(turned_s[m], y, NT, preferred_element_type=jnp.float32)
            for rr in range(RB):
                r = b * RB + rr
                at = slice(rr * W, (rr + 1) * W)
                q_s[r] = (p[:C, at] * HEAD_DIM ** (-0.5)).astype(jnp.bfloat16)
                v_s[r] = p[C : 2 * C, at].astype(jnp.bfloat16)
                g_s[r] = jax.nn.sigmoid(p[2 * C :, at])
            return carry

        lax.fori_loop(0, R // RB, chunk, 0)

    def turn_bias(g):
        per = JBLOCK // R
        for h in range(HEADS):
            for kb in range(W // JBLOCK):
                part = bias_s[0, kb * per : (kb + 1) * per, g, h].reshape(JBLOCK, W)
                bias_t[h, :, kb * JBLOCK : (kb + 1) * JBLOCK] = part.astype(jnp.float32).T.astype(
                    jnp.bfloat16
                )

    def row_gated(m, g, r):
        k = k_s[r]
        rows = []
        for jb in range(W // JBLOCK):
            at = slice(jb * JBLOCK, (jb + 1) * JBLOCK)
            q = q_s[r, :, at]
            head = lax.broadcasted_iota(jnp.int32, (C, JBLOCK), 0) // HEAD_DIM
            spread = jnp.concatenate(
                [jnp.where(head == h, q, jnp.zeros_like(q)) for h in range(HEADS)], axis=1
            )
            scores = dot32(k, spread)
            parts = []
            for h in range(HEADS):
                if m == 0:
                    bias = bias_t[h, :, at]
                else:
                    bias = bias_s[1, :, g, h, :, at].reshape(W, JBLOCK)
                s = scores[:, h * JBLOCK : (h + 1) * JBLOCK] + bias.astype(jnp.float32)
                top = jnp.max(s, 0, keepdims=True)
                weights = jnp.exp(s - top).astype(jnp.bfloat16)
                left = jnp.concatenate(
                    [
                        v_s[r, h * HEAD_DIM : (h + 1) * HEAD_DIM, :],
                        jnp.ones((16, W), jnp.bfloat16),
                    ],
                    axis=0,
                )
                summed = dot32(left, weights)
                parts.append(summed[:HEAD_DIM] / summed[HEAD_DIM : HEAD_DIM + 1])
            gated = jnp.concatenate(parts, axis=0) * g_s[r, :, at]
            rows.append(gated.T.astype(jnp.bfloat16))
        return rows[0] if len(rows) == 1 else jnp.concatenate(rows, axis=0)

    def attend(m, g, src):
        col = lax.broadcasted_iota(jnp.int32, (W, C), 0)
        length = length_of(g)
        weights = head_weights(1)

        def live_of(r):
            return col < jnp.where(first_row + r < length, length, 0)

        def chunk(b, carry):
            gated = [row_gated(m, g, b * RB + rr) for rr in range(RB)]
            joined = gated[0] if RB == 1 else jnp.concatenate(gated, axis=0)
            update = dot32(joined, wo_ref[m])
            done = []
            for rr in range(RB):
                r = b * RB + rr
                u = jnp.where(live_of(r), update[rr * W : (rr + 1) * W], 0.0)
                done.append((src[g, r].astype(jnp.float32) + u).astype(jnp.bfloat16))
            if m == 1:
                second = done[0] if RB == 1 else jnp.concatenate(done, axis=0)
                y = layer_norm(second, gain_ref[2:3, :], shift_ref[2:3, :])
                hidden = jnp.maximum(dot32(y, up_ref[...]), 0.0).astype(jnp.bfloat16)
                update = dot32(hidden, down_ref[...])
                for rr in range(RB):
                    r = b * RB + rr
                    u = jnp.where(live_of(r), update[rr * W : (rr + 1) * W], 0.0)
                    done[rr] = (done[rr].astype(jnp.float32) + u).astype(jnp.bfloat16)
            for rr in range(RB):
                r = b * RB + rr
                send_s[g, :, r] = done[rr].reshape(count, R, C)
                landed[m, g, first_row + r] = send_s[g, me, r]
            each_peer(lambda d: flip_copy(m, g, d, b * RB, RB).start())
            if m == 0:
                first = done[0] if RB == 1 else jnp.concatenate(done, axis=0)
                put_bias(weights, layer_norm(first, gain_ref[1:2, :], shift_ref[1:2, :]), b)
            return carry

        lax.fori_loop(0, R // RB, chunk, 0)

    def gather_flip(m, g, target):
        each_peer(lambda d: flip_copy(m, g, d, 0, R).wait_recv())

        def one(p, carry):
            rows = pl.ds(pl.multiple_of(p * R, R), R)
            tsc[p] = landed[m, g, rows].astype(jnp.float32)
            for c in range(R):
                target[g, c, rows, :] = tsc[p, :, c, :].astype(jnp.bfloat16)
            return carry

        lax.fori_loop(0, count, one, 0, unroll=count <= 8)

    column = lax.broadcasted_iota(jnp.int32, (R, W), 1)
    row = lax.broadcasted_iota(jnp.int32, (R, W), 0) + first_row

    def begin(g, carry):
        norm_bias(g)

        @pl.when(g == 0)
        def _():
            pl.semaphore_wait(barrier, count - 1)

        send_bias(0, g, column < length_of(g))
        return carry

    def start_node(g, carry):
        relay_bias(0, g)
        project(0, g)
        each_chip(0, lambda e: bias_copy(0, g, e, True).wait_recv())
        turn_bias(g)
        attend(0, g, x_ref)
        send_bias(1, g, row < length_of(g))
        return carry

    def end_node(g, carry):
        relay_bias(1, g)
        gather_flip(0, g, x1)
        project(1, g)
        each_chip(0, lambda e: bias_copy(1, g, e, True).wait_recv())
        each_peer(lambda d: flip_copy(0, g, d, 0, R).wait_send())
        attend(1, g, x1)
        return carry

    def finish(g, carry):
        gather_flip(1, g, out_ref)
        each_peer(lambda d: flip_copy(1, g, d, 0, R).wait_send())
        for m in range(2):
            each_chip(0, lambda e: bias_copy(m, g, e, True).wait_send())
            each_chip(1, lambda e: bias_copy(m, g, e, False).wait_send())
        return carry

    for m in range(2):
        for at, first in enumerate((0, 2 * C, 3 * C)):
            part = proj_ref[m, :, first : first + C].astype(jnp.float32)
            turned_s[m, at * C : (at + 1) * C, :] = part.T.astype(jnp.bfloat16)
    for stage in (begin, start_node, end_node, finish):
        lax.fori_loop(0, G, stage, 0)


def on_device(
    pair_state, lengths, norm_gain, norm_shift, attn_proj, bias_proj, attn_out, trans_up, trans_down
):
    G, R, W, C = pair_state.shape
    count = lax.axis_size("dap")
    RB = 8 if W <= 128 else 1
    wb = jnp.swapaxes(bias_proj, 1, 2)
    bf = jnp.bfloat16
    f32 = jnp.float32
    vm = pl.BlockSpec(memory_space=pltpu.VMEM)
    return pl.pallas_call(
        partial(kernel, (count, G, R, W, C, RB)),
        out_shape=jax.ShapeDtypeStruct((G, R, W, C), bf),
        in_specs=[pl.BlockSpec(memory_space=pltpu.SMEM)] + [vm] * 8,
        out_specs=vm,
        scratch_shapes=[
            pltpu.VMEM((G, R, W, C), bf),
            pltpu.VMEM((2, G, W, R, C), bf),
            pltpu.VMEM((G, R, W, C), bf),
            pltpu.VMEM((R, C, W), bf),
            pltpu.VMEM((R, W, C), bf),
            pltpu.VMEM((R, C, W), bf),
            pltpu.VMEM((R, C, W), f32),
            pltpu.VMEM((count, R, R, C), f32),
            pltpu.VMEM((R, 8, W), f32),
            pltpu.VMEM((HEADS, W, W), bf),
            pltpu.VMEM((2, 3 * C, C), bf),
            pltpu.VMEM((2, count, G, HEADS, R, W), bf),
            pltpu.VMEM((G, count, R, R, C), bf),
            pltpu.SemaphoreType.DMA((2, G, count)),
            pltpu.SemaphoreType.DMA((2, G, count)),
            pltpu.SemaphoreType.DMA((2, G, count)),
            pltpu.SemaphoreType.DMA((2, G, count)),
        ],
        compiler_params=pltpu.CompilerParams(
            collective_id=0, has_side_effects=True, vmem_limit_bytes=60 * 1024 * 1024
        ),
        name="evoformer_pair",
    )(lengths, pair_state, norm_gain, norm_shift, attn_proj, wb, attn_out, trans_up, trans_down)


def solution(mesh):
    in_specs = (P("grp", "dap", None, None), P(), P(), P(), P(), P(), P(), P(), P())
    out_specs = P("grp", "dap", None, None)
    return jax.shard_map(
        on_device, mesh=mesh, in_specs=in_specs, out_specs=out_specs, check_vma=False
    )
```
